256 devices in a mesh: dp: 2 (over core), ctx: 32 (over z, x), tensor: 4 (over y).
Axes of the slice: x: 4, y: 4, z: 8, core: 2. Of those that a mesh axis runs over, the one named last changes fastest.
Arguments:
- features: bfloat16 [2, 8192, 8192], P('dp', 'ctx', 'tensor'), may hold values from -500 to 500
- gate_in: bfloat16 [2, 8192, 8192], P('dp', 'ctx', 'tensor'), may hold values from -6 to 6
- segments: int32 [2, 8192], P('dp', 'ctx'), may hold values from 0 to 3, never falling along the last dimension, each value on 1 to 4096 neighbouring positions
- gain: float32 [8192], P('tensor'), may hold values from 0.25 to 1.75
- residue: float32 [512, 16], P('tensor'), may hold values from -4 to 4
- rates: float32 [512, 16], P('tensor'), may hold values from 0 to 1
- grad_out: bfloat16 [2, 8192, 8192], P('dp', 'ctx', 'tensor'), may hold values from -6 to 6
Outputs:
- mixed: bfloat16 [2, 8192, 8192], P('dp', 'ctx', 'tensor')
- grad_features: bfloat16 [2, 8192, 8192], P('dp', 'ctx', 'tensor')
- grad_gate: bfloat16 [2, 8192, 8192], P('dp', 'ctx', 'tensor')
- grad_residue: float32 [512, 16], P('tensor')
- grad_gain: float32 [8192], P('tensor')
The draws below stay inside these ranges and needn't reach their ends.
Inputs may be any that keep to these rules, and one draw needn't show every extreme that they name: `segments`: pair ids never fall along a sequence; each of the 4 ids covers 1 to 4096 positions, and one covers exactly 4096.
All inputs are finite; a program needn't handle non-finite values.
Results may differ from the reference program's by a relative error of at most 0.001.
Values sent between devices are 32-bit elements; how exact they have to be, the bound alone decides.
No kernel may reach another device: no remote copies, remote signals or barrier semaphores. Data moves between devices by JAX's collectives and lax.ppermute only.
A program may use at most 128 MiB of HBM per device.

```python
import math
import jax
import jax.numpy as jnp
import numpy as np
from jax import lax

D = 8192
GROUP = 16
MODES = 16
COUNT = 4
BATCH = 2
SEQ = 8192
GROUPS = 512


def draw_features(key, part):
    key = jax.random.fold_in(key, 11)
    key_base = jax.random.fold_in(key, 1)
    key_rows = jax.random.fold_in(key, 2)
    columns = jnp.exp(jnp.log(10.0) * jnp.arange(D, dtype=jnp.float32) / D)
    base = jnp.clip(jax.random.normal(key_base, (BATCH, SEQ, D), jnp.float32), -5.0, 5.0)
    row_scale = jnp.exp(jax.random.uniform(key_rows, (BATCH, SEQ, 1), jnp.float32, 0.0, jnp.log(10.0)))
    return (base * columns * row_scale).astype(jnp.bfloat16)


def draw_rates(key, part):
    key = jax.random.fold_in(key, 23)
    key_spread = jax.random.fold_in(key, 1)
    slowest = jnp.log(0.02 / SEQ)
    fastest = jnp.log(1.0 / 30.0)
    value = jax.random.uniform(key_spread, (GROUPS, MODES), jnp.float32, slowest, fastest)
    return jnp.exp(value)


def steps_of(own_key, dims, shards, least, largest):
    factor_of = 1.0
    for axis_at, shards_of in shards:
        steps = jax.random.uniform(jax.random.fold_in(jax.random.fold_in(own_key, 6), axis_at), (shards_of,), jnp.float32, least / len(shards), largest / len(shards))
        factor_of = factor_of * jnp.repeat(jnp.exp(steps), dims[axis_at] // shards_of).reshape((-1,) + (1,) * (len(dims) - 1 - axis_at))
    return factor_of


def profile(number_of, total, most, skew):
    loads = [(1 << 20) // math.isqrt(grade ** skew) + 1 for grade in range(2, number_of + 1)]
    rest, given = total - most - (number_of - 1), [1] * (number_of - 1)
    while rest > 0:
        free = [i for i in range(number_of - 1) if given[i] < most]
        whole, budget = sum([loads[i] for i in free]), rest
        for i in free:
            extra = min(most - given[i], max(1, budget * loads[i] // whole), rest)
            given[i] = given[i] + extra
            rest = rest - extra
    return np.array([most] + given)


def ragged_sizes(key, number_of, total, reach, lean):
    if number_of == 2:
        one = jax.random.randint(key, (), max(1, total - reach), min(reach, total - 1) + 1)
        return jnp.stack([one, total - one])
    tallies = jnp.asarray(profile(number_of, total, reach, lean), jnp.int32)
    pairs = (number_of - 1) // 2
    giver, receiver = tallies[1:1 + 2 * pairs:2], tallies[2:2 + 2 * pairs:2]
    margin = jnp.minimum(giver - 1, reach - receiver)
    passed = jax.random.randint(jax.random.fold_in(key, 1), (pairs,), 0, 1 << 20) % (margin + 1)
    tallies = tallies.at[1:1 + 2 * pairs:2].set(giver - passed).at[2:2 + 2 * pairs:2].set(receiver + passed)
    return tallies[jax.random.permutation(jax.random.fold_in(key, 2), number_of)]


def normal_values(stream_key, shape, scale, bound, split=(), kind=jnp.bfloat16):
    drawn = jax.random.normal(stream_key, shape, jnp.float32) * scale
    if len(split) > 0:
        drawn = steps_of(stream_key, shape, split, -0.22, 0.18) * drawn
    return jnp.clip(drawn, min=-bound, max=bound).astype(kind)


def setup_inputs(seed: int = 0) -> dict:
    arg_keys = jax.random.split(jax.random.key(seed), 8)
    return {
        "features": draw_features(jax.random.fold_in(arg_keys[7], 71), 0),
        "gate_in": normal_values(arg_keys[1], (BATCH, SEQ, D), 1.0, 6.0, ((0, 2), (1, 32), (2, 4))),
        "segments": jax.vmap(lambda own: jnp.searchsorted(jnp.cumsum(ragged_sizes(own, COUNT, SEQ, SEQ // 2, 0)), jnp.arange(SEQ), side="right"))(jax.random.split(arg_keys[2], BATCH)).reshape((BATCH, SEQ)).astype(jnp.int32),
        "gain": jnp.clip(1.0 + 0.15 * jax.random.normal(arg_keys[3], (D,), jnp.float32), 0.25, 1.75),
        "residue": normal_values(arg_keys[4], (GROUPS, MODES), 0.25, 4.0, ((0, 4),), jnp.float32),
        "rates": draw_rates(jax.random.fold_in(arg_keys[7], 71), 0),
        "grad_out": normal_values(arg_keys[6], (BATCH, SEQ, D), 1.0, 6.0, ((0, 2), (1, 32), (2, 4))),
    }


epsilon = 1e-06
highest_level = lax.Precision.HIGHEST

def reference(features, gate_in, segments, gain, residue, rates, grad_out):
    block_len = math.gcd(64, SEQ)
    block_count = SEQ // block_len
    group_count = D // GROUP
    lag_steps = jnp.arange(block_len, dtype=jnp.float32)
    decay_source = jnp.exp(-rates[:, :, None] * lag_steps[None, None, :])
    trailing_decay = jnp.exp(-rates[:, :, None] * (block_len - 1.0 - lag_steps)[None, None, :])
    block_decay = jnp.exp(-rates * block_len)
    row_index = jnp.arange(block_len, dtype=jnp.int32)
    distance = row_index[:, None] - row_index[None, :]
    causal = distance >= 0
    tap_index = jnp.clip(distance, 0, block_len - 1).astype(jnp.int32)
    id_blocks = jnp.transpose(segments.reshape(BATCH, block_count, block_len), (1, 0, 2))

    def split_blocks(array):
        return jnp.transpose(array.reshape(BATCH, block_count, block_len, D), (1, 0, 2, 3))

    def forward(feat_full, gate_full, gain_vec, residue_mat):
        weights = residue_mat * jnp.sqrt(-jnp.expm1(-2.0 * rates))
        taps = jnp.einsum('gr,grn->gn', weights, decay_source, precision=highest_level)
        toeplitz = jnp.where(causal[None], taps[:, tap_index], 0.0)
        reach_length = weights[:, :, None] * decay_source * jnp.exp(-rates)[:, :, None]

        def advance(carry, inputs):
            current_state, last_seen = carry
            feat_block, gate_block, id_block = inputs
            mean_square = lax.optimization_barrier(jnp.mean(feat_block * feat_block, axis=2, keepdims=True))
            normed = feat_block * lax.rsqrt(mean_square + epsilon) * gain_vec
            grouped_rows = normed.reshape(BATCH, block_len, group_count, GROUP)
            same_pair = (id_block[:, :, None] == id_block[:, None, :]).astype(jnp.float32)
            kernel = toeplitz[None] * same_pair[:, None]
            local_part = jnp.einsum('bgts,bsgc->btgc', kernel, grouped_rows, precision=highest_level)
            linked = (id_block == last_seen[:, None]).astype(jnp.float32)
            carried_over = jnp.einsum('eni,qepn->qiep', reach_length, current_state, precision=highest_level)
            conv = local_part + linked[:, :, None, None] * carried_over
            trailing_mask = (id_block == id_block[:, -1:]).astype(jnp.float32)
            fresh_value = jnp.einsum('we,zme,wezi->wzim', trailing_mask, trailing_decay, grouped_rows, precision=highest_level)
            passing = (id_block[:, -1] == last_seen).astype(jnp.float32)
            new_state = fresh_value + passing[:, None, None, None] * block_decay[None, :, None, :] * current_state
            gated = gate_block * conv.reshape(BATCH, block_len, D)
            return ((new_state, id_block[:, -1]), gated)
        start_state = jnp.zeros((BATCH, group_count, GROUP, MODES), jnp.float32)
        start_id = jnp.full((BATCH,), -1, jnp.int32)
        blocks_out = lax.scan(jax.checkpoint(advance), (start_state, start_id), (split_blocks(feat_full), split_blocks(gate_full), id_blocks))[1]
        return jnp.transpose(blocks_out, (1, 0, 2, 3)).reshape(BATCH, SEQ, D)
    feat_full = features.astype(jnp.float32)
    gate_full = gate_in.astype(jnp.float32)
    mixed_full, pullback = jax.vjp(forward, feat_full, gate_full, gain, residue)
    grad_feat, grad_gate_full, grad_gain_raw, grad_res_raw = pullback(grad_out.astype(jnp.float32))
    norm_factor = 1.0 / math.sqrt(BATCH * SEQ)
    return (mixed_full.astype(jnp.bfloat16), grad_feat.astype(jnp.bfloat16), grad_gate_full.astype(jnp.bfloat16), grad_res_raw * norm_factor, grad_gain_raw * norm_factor)
```

```python
import math

import jax
import jax.numpy as jnp
from jax import lax
from jax.experimental import pallas as pl
from jax.experimental.pallas import tpu as pltpu
from jax.sharding import PartitionSpec as P

epsilon = 1e-06
LANES = 128
TILES = 8
MODES = 16
GROUP = 16
UNROLL = 8
EXTRA = 8
HIGHEST = lax.Precision.HIGHEST
f32 = jnp.float32


def lane_iota(rows):
    return lax.broadcasted_iota(jnp.int32, (rows, LANES), 1)


def swap(value):
    return pltpu.roll(value, LANES // 2, axis=1)


def join(low, high):
    return jnp.where(lane_iota(low.shape[0]) < LANES // 2, low, high)


def column(row_ref, length):
    row = jnp.broadcast_to(row_ref[0:1, :], (8, length))
    return jnp.broadcast_to(jnp.transpose(row)[:, 0:1], (length, LANES))


def block_ones():
    left = lax.broadcasted_iota(jnp.int32, (LANES, LANES), 0) // GROUP
    right = lax.broadcasted_iota(jnp.int32, (LANES, LANES), 1) // GROUP
    return jnp.where(left == right, 1.0, 0.0).astype(f32)


def to_scan(dst, tile, value, length):
    dst[pl.ds(tile, length, stride=TILES), :] = value


def from_scan(src, tile, length):
    return src[pl.ds(tile, length, stride=TILES), :]


def tile_of(ref, tile):
    return ref[:, tile * LANES : (tile + 1) * LANES].astype(f32)


def tree(values):
    values = list(values)
    while len(values) > 1:
        values = [a + b for a, b in zip(values[::2], values[1::2])]
    return values[0]


def scan(length, seg, step, carry, backward):
    groups = length // UNROLL

    def body(index, carry):
        group = groups - 1 - index if backward else index
        base = group * UNROLL
        if backward:
            edge = jnp.minimum(base + UNROLL, length - 1)
            plain = seg[0, base] == seg[0, edge]
        else:
            edge = jnp.maximum(base - 1, 0)
            plain = seg[0, edge] == seg[0, base + UNROLL - 1]

        def fast(carry):
            for u in range(UNROLL):
                t = base + (UNROLL - 1 - u if backward else u)
                carry = step(t, carry, None)
            return carry

        def slow(carry):
            for u in range(UNROLL):
                t = base + (UNROLL - 1 - u if backward else u)
                near = jnp.minimum(t + 1, length - 1) if backward else jnp.maximum(t - 1, 0)
                carry = step(t, carry, seg[0, t] == seg[0, near])
            return carry

        return lax.cond(plain, fast, slow, carry)

    return lax.fori_loop(0, groups, body, carry)


def decayed(decay, state, keep):
    state = decay * state
    return state if keep is None else jnp.where(keep, state, 0.0)


def row_at(ref, t):
    return ref[pl.ds(pl.multiple_of(t * TILES, TILES), TILES), :]


def adjoint_kernel(seg, gate, grad, rates, adj, grad_scan):
    length = gate.shape[0]
    for tile in range(TILES):
        to_scan(grad_scan, tile, tile_of(gate, tile) * tile_of(grad, tile), length)
    decay = [jnp.exp(-rates[r]) for r in range(MODES)]

    def step(t, states, keep):
        value = row_at(grad_scan, t)
        return tuple(decayed(decay[r], states[r], keep) + value for r in range(MODES))

    zero = jnp.zeros((TILES, LANES), f32)
    states = scan(length, seg, step, (zero,) * MODES, True)
    for r in range(MODES):
        adj[pl.ds(r, TILES, stride=MODES), :] = states[r]


def state_kernel(
    seg, feats, gate, grad, inverse, rates, weights, gain, adj, msg, feat_scan, grad_scan, ends, sums
):
    length = gate.shape[0]
    scale = column(inverse, length)
    for tile in range(TILES):
        to_scan(feat_scan, tile, tile_of(feats, tile) * scale, length)
        to_scan(grad_scan, tile, tile_of(gate, tile) * tile_of(grad, tile), length)
    decay = [jnp.exp(-rates[r]) for r in range(MODES)]

    def step(t, carry, keep):
        value = row_at(feat_scan, t)
        grads = row_at(grad_scan, t)
        states = [decayed(decay[r], carry[r], keep) + value for r in range(MODES)]
        totals = [carry[MODES + r] + grads * states[r] for r in range(MODES)]
        return tuple(states) + tuple(totals)

    zero = jnp.zeros((TILES, LANES), f32)
    carry = scan(length, seg, step, (zero,) * (2 * MODES), False)
    gains = gain[...]
    for r in range(MODES):
        ends[pl.ds(r, TILES, stride=MODES), :] = carry[r]
        sums[r * TILES : (r + 1) * TILES, :] = carry[MODES + r] * gains
    gain_row = tree([weights[r] * carry[MODES + r] for r in range(MODES)])
    spread = jnp.dot(sums[...], block_ones(), precision=HIGHEST, preferred_element_type=f32)
    lane_mode = lane_iota(TILES) % GROUP
    mode_row = tree(
        [
            jnp.where(lane_mode == r, spread[r * TILES : (r + 1) * TILES, :], 0.0)
            for r in range(MODES)
        ]
    )
    even = join(gain_row, swap(mode_row))
    odd = join(swap(gain_row), mode_row)
    first = jnp.full((1, LANES), seg[0, 0], jnp.int32).astype(f32)
    last = jnp.full((1, LANES), seg[0, length - 1], jnp.int32).astype(f32)
    near = join(first, last)
    far = join(last, first)
    sub = lax.broadcasted_iota(jnp.int32, (EXTRA, LANES), 0)

    def extra(row):
        return jnp.where(sub == 0, near, jnp.where(sub == 1, far, jnp.where(sub == 2, row, 0.0)))

    for tile in range(TILES):
        state = ends[tile * MODES : (tile + 1) * MODES, :]
        adjoint = adj[tile * MODES : (tile + 1) * MODES, :]
        msg[2 * tile, 0:MODES, :] = join(state, swap(adjoint))
        msg[2 * tile + 1, 0:MODES, :] = join(swap(state), adjoint)
        msg[2 * tile, MODES:, :] = extra(even[tile : tile + 1, :])
        msg[2 * tile + 1, MODES:, :] = extra(odd[tile : tile + 1, :])


def carry_kernel(span, own, msg, rates, weights, gain, out, carries):
    count = msg.shape[0]
    tile = own[0] // 2
    odd = own[0] % 2 == 1
    tiles = gain.shape[0]

    def mine(value):
        other = swap(value)
        return jnp.where(odd, join(other, value), join(value, other))

    rate = mine(rates[pl.ds(tile, MODES, stride=tiles), :])
    weight = mine(weights[pl.ds(tile, MODES, stride=tiles), :])
    gains = mine(gain[pl.ds(tile, 1), :])
    single = jnp.exp(-rate)
    whole = jnp.exp(-rate * float(span))
    state = jnp.zeros((MODES, LANES), f32)
    before = None
    for m in range(count):
        fresh = join(msg[m, 0:MODES, :], msg[count - 1 - m, 0:MODES, :])
        near = join(msg[m, MODES : MODES + 1, :], msg[count - 1 - m, MODES : MODES + 1, :])
        far = join(msg[m, MODES + 1 : MODES + 2, :], msg[count - 1 - m, MODES + 1 : MODES + 2, :])
        if before is None:
            carries[m] = state
            state = fresh
        else:
            carries[m] = jnp.where(near == before, state, 0.0)
            state = fresh + jnp.where(far == before, whole * state, 0.0)
        before = far
    total = jnp.zeros((MODES, LANES), f32)
    row = jnp.zeros((1, LANES), f32)
    for i in range(count):
        carried = join(carries[i], carries[count - 1 - i])
        out[i, 0:MODES, :] = carried
        total = total + carried * swap(msg[i, 0:MODES, :])
        row = row + msg[i, MODES + 2 : MODES + 3, :]
    total = total * single
    gain_row = jnp.sum(weight * total, axis=0, keepdims=True)
    spread = jnp.dot(total * gains, block_ones(), precision=HIGHEST, preferred_element_type=f32)
    pick = lane_iota(MODES) % GROUP == lax.broadcasted_iota(jnp.int32, (MODES, LANES), 0)
    mode_row = jnp.sum(jnp.where(pick, spread, 0.0), axis=0, keepdims=True)
    row = row + join(gain_row, swap(mode_row))
    for i in range(count):
        out[i, MODES:, :] = jnp.broadcast_to(row, (EXTRA, LANES))


def load_carry(back, ends, ahead):
    for tile in range(TILES):
        low = back[2 * tile, 0:MODES, :]
        high = back[2 * tile + 1, 0:MODES, :]
        value = join(swap(low), high) if ahead else join(low, swap(high))
        ends[tile * MODES : (tile + 1) * MODES, :] = value
    return tuple(ends[pl.ds(r, TILES, stride=MODES), :] for r in range(MODES))


def backward_kernel(
    seg, back, feats, gate, grad, rates, weights, gain, scaled, inner, grad_scan, result, ends
):
    length = gate.shape[0]
    for tile in range(TILES):
        to_scan(grad_scan, tile, tile_of(gate, tile) * tile_of(grad, tile), length)
    decay = [jnp.exp(-rates[r]) for r in range(MODES)]
    weight = [weights[r] for r in range(MODES)]

    def step(t, states, keep):
        value = row_at(grad_scan, t)
        states = tuple(decayed(decay[r], states[r], keep) + value for r in range(MODES))
        result[pl.ds(pl.multiple_of(t * TILES, TILES), TILES), :] = tree(
            [weight[r] * states[r] for r in range(MODES)]
        )
        return states

    scan(length, seg, step, load_carry(back, ends, True), True)
    partial = jnp.zeros((length, LANES), f32)
    for tile in range(TILES):
        value = from_scan(result, tile, length) * gain[tile : tile + 1, :]
        scaled[:, tile * LANES : (tile + 1) * LANES] = value
        partial = partial + value * tile_of(feats, tile)
    row = lax.dot_general(
        jnp.ones((8, LANES), f32),
        partial,
        (((1,), (1,)), ((), ())),
        precision=HIGHEST,
        preferred_element_type=f32,
    )

    @pl.when(pl.program_id(0) == 0)
    def _():
        inner[...] = row

    @pl.when(pl.program_id(0) != 0)
    def _():
        inner[...] += row


def forward_kernel(
    seg, back, feats, gate, grad, inverse, rates, weights, gain, mixed, grad_gate, feat_scan, result, ends
):
    length = gate.shape[0]
    scale = column(inverse, length)
    for tile in range(TILES):
        to_scan(feat_scan, tile, tile_of(feats, tile) * scale, length)
    decay = [jnp.exp(-rates[r]) for r in range(MODES)]
    weight = [weights[r] for r in range(MODES)]

    def step(t, states, keep):
        value = row_at(feat_scan, t)
        states = tuple(decayed(decay[r], states[r], keep) + value for r in range(MODES))
        result[pl.ds(pl.multiple_of(t * TILES, TILES), TILES), :] = tree(
            [weight[r] * states[r] for r in range(MODES)]
        )
        return states

    scan(length, seg, step, load_carry(back, ends, False), False)
    for tile in range(TILES):
        conv = from_scan(result, tile, length) * gain[tile : tile + 1, :]
        at = slice(tile * LANES, (tile + 1) * LANES)
        mixed[:, at] = (tile_of(gate, tile) * conv).astype(jnp.bfloat16)
        grad_gate[:, at] = (tile_of(grad, tile) * conv).astype(jnp.bfloat16)


def feature_kernel(full_width, scaled, feats, inverse, inner, out):
    length = feats.shape[0]
    scale = column(inverse, length)
    factor = column(inner, length) * scale * scale / full_width
    for tile in range(feats.shape[1] // LANES):
        at = slice(tile * LANES, (tile + 1) * LANES)
        out[:, at] = (scale * (scaled[:, at] - tile_of(feats, tile) * factor)).astype(jnp.bfloat16)


def params():
    return pltpu.CompilerParams(vmem_limit_bytes=24 * 1024 * 1024)


def cost(flops, moved):
    return pl.CostEstimate(flops=flops, bytes_accessed=moved, transcendentals=0)


def sum_tensor(value):
    size = lax.axis_size("tensor")
    total = value
    for d in range(1, size):
        total = total + lax.ppermute(value, "tensor", [(i, (i + d) % size) for i in range(size)])
    return total


def shards(features, gate_in, segments, gain, residue, rates, grad_out):
    _, length, width = features.shape
    group_count, mode_count = rates.shape
    count = lax.axis_size("ctx")
    full_width = width * lax.axis_size("tensor")
    tiles = width // LANES
    halves = tiles // TILES
    half = TILES * LANES
    feat2 = features[0]
    gate2 = gate_in[0]
    grad2 = grad_out[0]

    feats = features.astype(f32)
    square_sum = sum_tensor(jnp.sum(feats * feats, axis=2))
    inverse = lax.rsqrt(square_sum / full_width + epsilon)

    root_weight = jnp.sqrt(-jnp.expm1(-2.0 * rates))
    tables = jnp.stack([rates, residue * root_weight])
    tables = jnp.transpose(tables, (0, 2, 1)).reshape(2, mode_count, tiles, LANES // GROUP)
    tables = jnp.broadcast_to(tables[..., None], tables.shape + (GROUP,))
    tables = tables.reshape(2, mode_count, tiles, LANES)
    rate_table, weight_table = tables[0], tables[1]
    gain_table = gain.reshape(tiles, LANES)

    whole = pl.BlockSpec((length, half), lambda h: (0, h))
    table = pl.BlockSpec((mode_count, TILES, LANES), lambda h: (0, h, 0))
    gains = pl.BlockSpec((TILES, LANES), lambda h: (h, 0))
    states = pl.BlockSpec((TILES * MODES, LANES), lambda h: (h, 0))
    message = pl.BlockSpec((2 * TILES, MODES + EXTRA, LANES), lambda h: (h, 0, 0))
    vector = pl.BlockSpec((1, length), lambda h: (0, 0))
    ids = pl.BlockSpec(memory_space=pltpu.SMEM)
    scan_scratch = pltpu.VMEM((length * TILES, LANES), f32)
    state_scratch = pltpu.VMEM((TILES * MODES, LANES), f32)
    work = length * width * MODES

    adjoint = pl.pallas_call(
        adjoint_kernel,
        grid=(halves,),
        in_specs=[ids, whole, whole, table],
        out_specs=states,
        out_shape=jax.ShapeDtypeStruct((tiles * MODES, LANES), f32),
        scratch_shapes=[scan_scratch],
        compiler_params=params(),
        cost_estimate=cost(2 * work, 4 * length * width),
        name="adjoint",
    )(segments, gate2, grad2, rate_table)

    msg = pl.pallas_call(
        state_kernel,
        grid=(halves,),
        in_specs=[ids, whole, whole, whole, vector, table, table, gains, states],
        out_specs=message,
        out_shape=jax.ShapeDtypeStruct((count, MODES + EXTRA, LANES), f32),
        scratch_shapes=[scan_scratch, scan_scratch, state_scratch, state_scratch],
        compiler_params=params(),
        cost_estimate=cost(4 * work, 6 * length * width),
        name="states",
    )(segments, feat2, gate2, grad2, inverse, rate_table, weight_table, gain_table, adjoint)

    msg = lax.all_to_all(msg, "ctx", 0, 0, tiled=True)

    own = lax.axis_index("ctx").astype(jnp.int32).reshape(1)
    vmem = pl.BlockSpec(memory_space=pltpu.VMEM)
    flat = (mode_count * tiles, LANES)
    back = pl.pallas_call(
        lambda *refs: carry_kernel(length, *refs),
        in_specs=[ids, vmem, vmem, vmem, vmem],
        out_specs=vmem,
        out_shape=jax.ShapeDtypeStruct((count, MODES + EXTRA, LANES), f32),
        scratch_shapes=[pltpu.VMEM((count, MODES, LANES), f32)],
        compiler_params=params(),
        name="carries",
    )(own, msg, rate_table.reshape(flat), weight_table.reshape(flat), gain_table)

    back = lax.all_to_all(back, "ctx", 0, 0, tiled=True)

    scaled, inner = pl.pallas_call(
        backward_kernel,
        grid=(halves,),
        in_specs=[ids, message, whole, whole, whole, table, table, gains],
        out_specs=[whole, pl.BlockSpec((8, length), lambda h: (0, 0))],
        out_shape=[
            jax.ShapeDtypeStruct((length, width), f32),
            jax.ShapeDtypeStruct((8, length), f32),
        ],
        scratch_shapes=[scan_scratch, scan_scratch, state_scratch],
        compiler_params=params(),
        cost_estimate=cost(4 * work, 10 * length * width),
        name="backward",
    )(segments, back, feat2, gate2, grad2, rate_table, weight_table, gain_table)
    inner = sum_tensor(inner[0:1])

    mixed, grad_gate = pl.pallas_call(
        forward_kernel,
        grid=(halves,),
        in_specs=[ids, message, whole, whole, whole, vector, table, table, gains],
        out_specs=[whole, whole],
        out_shape=[jax.ShapeDtypeStruct((length, width), jnp.bfloat16)] * 2,
        scratch_shapes=[scan_scratch, scan_scratch, state_scratch],
        compiler_params=params(),
        cost_estimate=cost(4 * work, 10 * length * width),
        name="forward",
    )(segments, back, feat2, gate2, grad2, inverse, rate_table, weight_table, gain_table)

    grad_features = pl.pallas_call(
        lambda *refs: feature_kernel(full_width, *refs),
        grid=(halves,),
        in_specs=[whole, whole, vector, vector],
        out_specs=whole,
        out_shape=jax.ShapeDtypeStruct((length, width), jnp.bfloat16),
        compiler_params=params(),
        cost_estimate=cost(4 * length * width, 8 * length * width),
        name="features",
    )(scaled, feat2, inverse, inner)

    totals = back[:, MODES, :]
    size = lax.axis_size("dp")
    for d in range(1, size):
        totals = totals + lax.ppermute(
            back[:, MODES, :], "dp", [(i, (i + d) % size) for i in range(size)]
        )
    norm_factor = 1.0 / math.sqrt(size * length * count)
    grad_gain = totals[:, : LANES // 2].reshape(width) * norm_factor
    mode_total = totals[:, LANES // 2 :].reshape(group_count, mode_count)
    return (
        mixed[None],
        grad_features[None],
        grad_gate[None],
        mode_total * root_weight * norm_factor,
        grad_gain,
    )


def solution(mesh):
    placed = (
        P("dp", "ctx", "tensor"),
        P("dp", "ctx", "tensor"),
        P("dp", "ctx"),
        P("tensor"),
        P("tensor", None),
        P("tensor", None),
        P("dp", "ctx", "tensor"),
    )
    return jax.shard_map(
        shards,
        mesh=mesh,
        in_specs=placed,
        out_specs=(
            P("dp", "ctx", "tensor"),
            P("dp", "ctx", "tensor"),
            P("dp", "ctx", "tensor"),
            P("tensor", None),
            P("tensor"),
        ),
        check_vma=False,
    )
```

```python
import math

import jax
import jax.numpy as jnp
from jax import lax
from jax.experimental import pallas as pl
from jax.experimental.pallas import tpu as pltpu
from jax.sharding import PartitionSpec as P

epsilon = 1e-06
LANES = 128
TILES = 8
HALVES = 2
MODES = 16
GROUP = 16
UNROLL = 16
COUNT = 4
COPIES = 8
WIDE = 2 * LANES
EXTRA = 8
HIGHEST = lax.Precision.HIGHEST
f32 = jnp.float32


def lane_iota(rows):
    return lax.broadcasted_iota(jnp.int32, (rows, LANES), 1)


def swap(value):
    return pltpu.roll(value, LANES // 2, axis=1)


def join(low, high):
    return jnp.where(lane_iota(low.shape[0]) < LANES // 2, low, high)


def total_row(parts):
    return tree([part[...] for part in parts])


def inverse_of(parts, full_width):
    return lax.rsqrt(total_row(parts) / full_width + epsilon)


def column(row):
    length = row.shape[1]
    row = jnp.broadcast_to(row, (8, length))
    return jnp.broadcast_to(jnp.transpose(row)[:, 0:1], (length, LANES))


def block_ones():
    left = lax.broadcasted_iota(jnp.int32, (LANES, LANES), 0) // GROUP
    right = lax.broadcasted_iota(jnp.int32, (LANES, LANES), 1) // GROUP
    return jnp.where(left == right, 1.0, 0.0).astype(f32)


def lanes_of(half, tile):
    return pl.ds(pl.multiple_of((half * TILES + tile) * LANES, LANES), LANES)


def tile_of(ref, half, tile):
    return ref[:, lanes_of(half, tile)].astype(f32)


def scan_rows(half, tile, length):
    return pl.ds(half * length * TILES + tile, length, stride=TILES)


def table_of(table, half, first):
    at = pl.ds(pl.multiple_of(half * TILES, TILES), TILES)
    return [table[first + r, at, :] for r in range(MODES)]


def decay_of(table, half):
    return [jnp.exp(-rate) for rate in table_of(table, half, 0)]


def weight_of(table, half):
    return table_of(table, half, MODES)


def state_rows(half, r):
    return pl.ds(half * TILES * MODES + r, TILES, stride=MODES)


def tree(values):
    values = list(values)
    while len(values) > 1:
        values = [a + b for a, b in zip(values[::2], values[1::2])]
    return values[0]


def scan(length, seg, cuts, step, carry, backward):
    groups = length // UNROLL

    def run(group, carry, masked):
        base = group * UNROLL
        for u in range(UNROLL):
            t = base + (UNROLL - 1 - u if backward else u)
            keep = None
            if masked:
                near = jnp.minimum(t + 1, length - 1) if backward else jnp.maximum(t - 1, 0)
                keep = seg[0, t] == seg[0, near]
            carry = step(t, carry, keep)
        return carry

    def stretch(p, carry):
        now, states = carry
        if backward:
            cut = jnp.where(p < COUNT - 1, cuts[jnp.maximum(COUNT - 2 - p, 0)], 0)
            group = (cut - 1) // UNROLL
            stop = jnp.where(
                cut >= length, now, jnp.where(cut <= 0, 0, jnp.minimum(now, group + 1))
            )
            states = lax.fori_loop(
                0, now - stop, lambda i, value: run(now - 1 - i, value, False), states
            )
            broken = (cut > 0) & (cut < length) & (group < now)
            after = group
        else:
            cut = jnp.where(p < COUNT - 1, cuts[jnp.minimum(p, COUNT - 2)], length)
            group = cut // UNROLL
            stop = jnp.where(
                cut <= 0, now, jnp.where(cut >= length, groups, jnp.maximum(now, group))
            )
            states = lax.fori_loop(now, stop, lambda i, value: run(i, value, False), states)
            broken = (cut > 0) & (cut < length) & (group >= now)
            after = group + 1
        states = lax.cond(
            broken, lambda value: run(group, value, True), lambda value: value, states
        )
        return jnp.where(broken, after, stop), states

    start = jnp.int32(groups if backward else 0)
    return lax.fori_loop(0, COUNT, stretch, (start, carry))[1]


def decayed(decay, state, keep):
    state = decay * state
    return state if keep is None else jnp.where(keep, state, 0.0)


def row_at(ref, half, length, t):
    return ref[pl.ds(pl.multiple_of((half * length + t) * TILES, TILES), TILES), :]


def lane_sums(value):
    return lax.dot_general(
        jnp.ones((8, LANES), f32),
        value,
        (((1,), (1,)), ((), ())),
        precision=HIGHEST,
        preferred_element_type=f32,
    )[0:1]


def load_kernel(
    feats_in, gate_in, grad_in, rates_in, residue_in, seg_in,
    feats, grad_scan, squares, table, cuts,
    gate, grad, rates, residue, seg, sems, small_sems,
):
    length, width = feats.shape
    step = length // COPIES
    small = [
        pltpu.make_async_copy(src, dst, small_sems.at[n])
        for n, (src, dst) in enumerate(((rates_in, rates), (residue_in, residue), (seg_in, seg)))
    ]
    copies = []
    for n, (src, dst) in enumerate(((feats_in, feats), (gate_in, gate), (grad_in, grad))):
        for i in range(COPIES):
            at = pl.ds(i * step, step)
            copies.append(pltpu.make_async_copy(src.at[at, :], dst.at[at, :], sems.at[n, i]))
    for copy in small + copies:
        copy.start()
    for copy in small:
        copy.wait()
    expand(rates, residue, seg, table, cuts)
    for i in range(COPIES):
        copies[i].wait()
    partial = jnp.zeros((length, LANES), f32)
    for tile in range(width // LANES):
        value = tile_of(feats, 0, tile)
        partial = partial + value * value
    squares[...] = lane_sums(partial)
    for copy in copies[COPIES:]:
        copy.wait()
    for half in range(HALVES):
        for tile in range(TILES):
            value = tile_of(gate, half, tile) * tile_of(grad, half, tile)
            grad_scan[scan_rows(half, tile, length), :] = value


def mode_params(rates, residue):
    rate = rates[...]
    twice = 2.0 * rate
    series = 1.0 - twice / 6.0
    for n in (5, 4, 3, 2):
        series = 1.0 - twice / n * series
    root = jnp.sqrt(jnp.where(twice < 0.25, twice * series, 1.0 - jnp.exp(-twice)))
    return jnp.concatenate([rate, residue[...] * root, root], axis=0)


def spread_groups(packed, width, first):
    group_count = packed.shape[1]
    group = lax.broadcasted_iota(jnp.int32, (group_count, width), 0)
    lane = lax.broadcasted_iota(jnp.int32, (group_count, width), 1)
    spread = jnp.where(first(lane) == group, 1.0, 0.0).astype(f32)
    return jnp.dot(packed, spread, precision=HIGHEST, preferred_element_type=f32)


def own_mode(value):
    row = lax.broadcasted_iota(jnp.int32, value.shape, 0)
    lane = lax.broadcasted_iota(jnp.int32, value.shape, 1)
    return jnp.sum(jnp.where(row == lane % GROUP, value, 0.0), axis=0, keepdims=True)


def expand(rates, residue, seg, table, cuts):
    width = table.shape[1] * LANES
    full = spread_groups(mode_params(rates, residue), width, lambda lane: lane // GROUP)
    for tile in range(width // LANES):
        at = slice(tile * LANES, (tile + 1) * LANES)
        table[:, tile, :] = full[0 : 2 * MODES, at]
    for p in range(COUNT - 1):
        cuts[p] = jnp.sum(jnp.where(seg[...] <= p, 1, 0))
    cuts[COUNT - 1] = seg.shape[1]


def adjoint_kernel(seg, cuts, grad_scan, table, adj):
    length = seg.shape[1]

    def run(half, _):
        decay = decay_of(table, half)

        def step(t, states, keep):
            value = row_at(grad_scan, half, length, t)
            return tuple(decayed(decay[r], states[r], keep) + value for r in range(MODES))

        zero = jnp.zeros((TILES, LANES), f32)
        states = scan(length, seg, cuts, step, (zero,) * MODES, True)
        for r in range(MODES):
            adj[state_rows(half, r), :] = states[r]
        return _

    lax.fori_loop(0, HALVES, run, 0)


def state_kernel(
    full_width, seg, cuts, feats, grad_scan, part0, part1, part2, part3, table, gain, adj,
    msg_out, inverse, msg, feat_scan, ends, sums, sems,
):
    length = feats.shape[0]
    inverse[...] = inverse_of((part0, part1, part2, part3), full_width)
    scale = column(inverse[...])
    share = msg.shape[0] // HALVES

    def send(half):
        at = pl.ds(half * share, share)
        return pltpu.make_async_copy(msg.at[at], msg_out.at[at], sems.at[half])

    for half in range(HALVES):
        state_half(
            length, half, scale, seg, cuts, feats, grad_scan, table, gain, adj,
            msg, feat_scan, ends, sums,
        )
        send(half).start()
    for half in range(HALVES):
        send(half).wait()


def state_half(
    length, half, scale, seg, cuts, feats, grad_scan, table, gain, adj,
    msg, feat_scan, ends, sums,
):
    for tile in range(TILES):
        feat_scan[scan_rows(0, tile, length), :] = tile_of(feats, half, tile) * scale
    decay = decay_of(table, half)

    def step(t, carry, keep):
        value = row_at(feat_scan, 0, length, t)
        grads = row_at(grad_scan, half, length, t)
        states = [decayed(decay[r], carry[r], keep) + value for r in range(MODES)]
        totals = [carry[MODES + r] + grads * states[r] for r in range(MODES)]
        return tuple(states) + tuple(totals)

    zero = jnp.zeros((TILES, LANES), f32)
    carry = scan(length, seg, cuts, step, (zero,) * (2 * MODES), False)
    gains = gain[pl.ds(pl.multiple_of(half * TILES, TILES), TILES), :]
    weights = weight_of(table, half)
    for r in range(MODES):
        ends[pl.ds(r, TILES, stride=MODES), :] = carry[r]
        sums[r * TILES : (r + 1) * TILES, :] = carry[MODES + r] * gains
    gain_row = tree([weights[r] * carry[MODES + r] for r in range(MODES)])
    spread = jnp.dot(sums[...], block_ones(), precision=HIGHEST, preferred_element_type=f32)
    lane_mode = lane_iota(TILES) % GROUP
    mode_row = tree(
        [
            jnp.where(lane_mode == r, spread[r * TILES : (r + 1) * TILES, :], 0.0)
            for r in range(MODES)
        ]
    )
    even = join(gain_row, swap(mode_row))
    odd = join(swap(gain_row), mode_row)
    first = jnp.full((1, LANES), seg[0, 0], jnp.int32).astype(f32)
    last = jnp.full((1, LANES), seg[0, length - 1], jnp.int32).astype(f32)
    near = join(first, last)
    far = join(last, first)
    sub = lax.broadcasted_iota(jnp.int32, (EXTRA, LANES), 0)

    def extra(row):
        return jnp.where(sub == 0, near, jnp.where(sub == 1, far, jnp.where(sub == 2, row, 0.0)))

    for tile in range(TILES):
        state = ends[tile * MODES : (tile + 1) * MODES, :]
        own = (half * TILES + tile) * MODES
        adjoint = adj[pl.ds(pl.multiple_of(own, MODES), MODES), :]
        at = 2 * (half * TILES + tile)
        msg[at, 0:MODES, :] = join(state, swap(adjoint))
        msg[at + 1, 0:MODES, :] = join(swap(state), adjoint)
        msg[at, MODES:, :] = extra(even[tile : tile + 1, :])
        msg[at + 1, MODES:, :] = extra(odd[tile : tile + 1, :])


def carry_kernel(
    span, norm_factor, own, msg, rates, residue, gain, out_hbm, out, carries, sems
):
    count = msg.shape[0]
    share = rates.shape[1] // count
    first = own[0] * share
    full = spread_groups(
        mode_params(rates, residue), LANES, lambda lane: first + lane % (LANES // 2) // GROUP
    )
    rate, weight = full[0:MODES], full[MODES : 2 * MODES]
    root = own_mode(full[2 * MODES :])
    at = pl.ds(pl.multiple_of(own[0] // 2 * LANES, LANES), LANES)
    gains = gain[:, at]
    odd = own[0] % 2 == 1
    gains = jnp.where(odd, join(swap(gains), gains), join(gains, swap(gains)))
    single = jnp.exp(-rate)
    whole = jnp.exp(-rate * float(span))
    state = jnp.zeros((MODES, LANES), f32)
    before = None
    for m in range(count):
        fresh = join(msg[m, 0:MODES, :], msg[count - 1 - m, 0:MODES, :])
        near = join(msg[m, MODES : MODES + 1, :], msg[count - 1 - m, MODES : MODES + 1, :])
        far = join(msg[m, MODES + 1 : MODES + 2, :], msg[count - 1 - m, MODES + 1 : MODES + 2, :])
        if before is None:
            carries[m] = state
            state = fresh
        else:
            carries[m] = jnp.where(near == before, state, 0.0)
            state = fresh + jnp.where(far == before, whole * state, 0.0)
        before = far
    total = jnp.zeros((MODES, LANES), f32)
    row = jnp.zeros((1, LANES), f32)
    for i in range(count):
        carried = join(carries[i], carries[count - 1 - i])
        out[i, 0:MODES, :] = carried
        total = total + carried * swap(msg[i, 0:MODES, :])
        row = row + msg[i, MODES + 2 : MODES + 3, :]
    total = total * single
    gain_row = jnp.sum(weight * total, axis=0, keepdims=True)
    spread = jnp.dot(total * gains, block_ones(), precision=HIGHEST, preferred_element_type=f32)
    pick = lane_iota(MODES) % GROUP == lax.broadcasted_iota(jnp.int32, (MODES, LANES), 0)
    mode_row = jnp.sum(jnp.where(pick, spread, 0.0), axis=0, keepdims=True)
    row = (row + join(gain_row, swap(mode_row))) * join(jnp.ones((1, LANES), f32), root)
    row = row * norm_factor
    modes = join(own_mode(rate), own_mode(weight))
    sub = lax.broadcasted_iota(jnp.int32, (EXTRA, LANES), 0)
    for i in range(count):
        out[i, MODES:, :] = jnp.where(sub == 0, row, modes)
    copies = []
    part = count // COPIES
    for i in range(COPIES):
        at = pl.ds(i * part, part)
        copies.append(pltpu.make_async_copy(out.at[at], out_hbm.at[at], sems.at[i]))
        copies[-1].start()
    for copy in copies:
        copy.wait()


def local_kernel(backward, seg, cuts, source, table, *refs):
    if backward:
        out, result, value_out, sems = refs
    else:
        inverse, out, result, value_out, sems, scan_in = refs
    length = seg.shape[1]
    scale = None if backward else column(inverse[...])
    copies = []
    for half in range(HALVES):
        if backward:
            values, at_half = source, half
        else:
            values, at_half = scan_in, 0
            for tile in range(TILES):
                values[scan_rows(0, tile, length), :] = tile_of(source, half, tile) * scale
        decay = decay_of(table, half)
        weight = weight_of(table, half)

        def step(t, states, keep):
            value = row_at(values, at_half, length, t)
            states = tuple(decayed(decay[r], states[r], keep) + value for r in range(MODES))
            result[pl.ds(pl.multiple_of(t * TILES, TILES), TILES), :] = tree(
                [weight[r] * states[r] for r in range(MODES)]
            )
            return states

        zero = jnp.zeros((TILES, LANES), f32)
        scan(length, seg, cuts, step, (zero,) * MODES, backward)
        for tile in range(TILES):
            value_out[:, lanes_of(half, tile)] = result[pl.ds(tile, length, stride=TILES), :]
        at = pl.ds(half * TILES * LANES, TILES * LANES)
        copies.append(pltpu.make_async_copy(value_out.at[:, at], out.at[:, at], sems.at[half]))
        copies[-1].start()
    wait_all(copies)


def from_owners(back, pair, rows, upper):
    parts = []
    for n in range(2):
        low = back[4 * pair + 2 * n, rows, :]
        high = back[4 * pair + 2 * n + 1, rows, :]
        parts.append(join(swap(low), high) if upper else join(low, swap(high)))
    return jnp.concatenate(parts, axis=1)


def powers(cuts, back, pair, length, ahead):
    t = lax.broadcasted_iota(jnp.int32, (length, WIDE), 0)
    modes = slice(MODES + 1, MODES + 2)
    rate = from_owners(back, pair, modes, False)
    weight = from_owners(back, pair, modes, True)
    sub = lax.broadcasted_iota(jnp.int32, (8, WIDE), 0).astype(f32)
    further = jnp.exp(-8.0 * rate)
    if ahead:
        edge = jnp.int32(0)
        for p in range(COUNT - 1):
            edge = jnp.maximum(edge, jnp.where(cuts[p] < length, cuts[p], 0))
        linked = t >= edge
        lag = 8.0 - sub
    else:
        edge = jnp.int32(length)
        for p in range(COUNT - 1):
            edge = jnp.minimum(edge, jnp.where(cuts[p] > 0, cuts[p], length))
        linked = t < edge
        lag = sub + 1.0
    blocks = [jnp.exp(-lag * rate) * weight]
    for _ in range(length // 8 - 1):
        blocks.append(blocks[-1] * further)
    power = jnp.concatenate(blocks[::-1] if ahead else blocks, axis=0)
    return split(jnp.where(linked, power, 0.0))


def split(value):
    high = value.astype(jnp.bfloat16)
    return high, (value - high.astype(f32)).astype(jnp.bfloat16)


def from_carry(cuts, back, pair, length, ahead):
    carry = from_owners(back, pair, slice(0, MODES), ahead)
    own = lax.broadcasted_iota(jnp.int32, (WIDE, WIDE), 0) // MODES == (
        lax.broadcasted_iota(jnp.int32, (WIDE, WIDE), 1) // GROUP
    )

    def spread(value):
        value = jnp.concatenate([value.astype(f32)] * (WIDE // MODES), axis=0)
        return jnp.where(own, value, 0.0).astype(jnp.bfloat16)

    high, low = (spread(value) for value in split(carry))
    near, far = powers(cuts, back, pair, length, ahead)
    dot = lambda x, y: jnp.dot(x, y, preferred_element_type=f32)
    return dot(near, high) + (dot(far, high) + dot(near, low))


def row_copies(src, dst, sems):
    step = dst.shape[0] // COPIES
    copies = []
    for i in range(COPIES):
        at = pl.ds(i * step, step)
        copies.append(pltpu.make_async_copy(src.at[at, :], dst.at[at, :], sems.at[i]))
        copies[-1].start()
    return copies


def wait_all(copies):
    for copy in copies:
        copy.wait()


def tiles_at(width):
    return [slice(tile * LANES, (tile + 1) * LANES) for tile in range(width // LANES)]


def backward_kernel(
    cuts, back, local_in, feats, gain, scaled, inner, totals, partial, local, sems
):
    length, width = feats.shape
    copies = row_copies(local_in, local, sems)
    for n in range(back.shape[0]):
        totals[n : n + 1, :] = back[n, MODES : MODES + 1, :]
    for pair in range(width // WIDE):
        at = slice(pair * WIDE, (pair + 1) * WIDE)
        scaled[:, at] = from_carry(cuts, back, pair, length, True)
    step = length // COPIES
    for i in range(COPIES):
        copies[i].wait()
        here = slice(i * step, (i + 1) * step)
        sums = []
        for at in tiles_at(width):
            value = (local[here, at] + scaled[here, at]) * gain[:, at]
            scaled[here, at] = value
            sums.append(value * feats[here, at].astype(f32))
        partial[here, :] = tree(sums)
    inner[...] = lane_sums(partial[...])


def forward_kernel(
    cuts, back, local, gate, grad_in, gain, mixed, grad_gate,
    carried, grad, mixed_v, grad_gate_v, sems, sems_in,
):
    length, width = gate.shape
    copies_in = row_copies(grad_in, grad, sems_in)
    for pair in range(width // WIDE):
        at = slice(pair * WIDE, (pair + 1) * WIDE)
        carried[:, at] = from_carry(cuts, back, pair, length, False)
    copies = []
    step = length // COPIES
    for i in range(COPIES):
        copies_in[i].wait()
        here = slice(i * step, (i + 1) * step)
        for at in tiles_at(width):
            conv = (local[here, at] + carried[here, at]) * gain[:, at]
            mixed_v[here, at] = (gate[here, at].astype(f32) * conv).astype(jnp.bfloat16)
            grad_gate_v[here, at] = (grad[here, at].astype(f32) * conv).astype(jnp.bfloat16)
        at = pl.ds(i * step, step)
        for n, (src, dst) in enumerate(((mixed_v, mixed), (grad_gate_v, grad_gate))):
            copies.append(pltpu.make_async_copy(src.at[at, :], dst.at[at, :], sems.at[n, i]))
            copies[-1].start()
    wait_all(copies)


def feature_kernel(
    full_width, scaled, feats, inverse, i0, i1, i2, i3, own, other,
    out, modes, gains, out_v, sems,
):
    length, width = feats.shape
    scale = column(inverse[...])
    factor = column(total_row((i0, i1, i2, i3))) * scale * scale / full_width
    copies = []
    step = length // COPIES
    for i in range(COPIES):
        here = slice(i * step, (i + 1) * step)
        for at in tiles_at(width):
            value = scale[here] * (scaled[here, at] - feats[here, at].astype(f32) * factor[here])
            out_v[here, at] = value.astype(jnp.bfloat16)
        at = pl.ds(i * step, step)
        copies.append(pltpu.make_async_copy(out_v.at[at, :], out.at[at, :], sems.at[i]))
        copies[-1].start()

    total = own[...] + other[...]
    count = total.shape[0]
    groups = modes.shape[1]
    share = groups // count
    slot = lax.broadcasted_iota(jnp.int32, (count, groups), 1) // share
    pick = jnp.where(slot == lax.broadcasted_iota(jnp.int32, (count, groups), 0), 1.0, 0.0)
    spread = lax.dot_general(
        total,
        pick.astype(f32),
        (((0,), (0,)), ((), ())),
        precision=HIGHEST,
        preferred_element_type=f32,
    )
    member = lax.broadcasted_iota(jnp.int32, (MODES, groups), 1) % share
    parts = [
        jnp.where(member == n, spread[LANES // 2 + n * MODES : LANES // 2 + (n + 1) * MODES], 0.0)
        for n in range(share)
    ]
    modes[...] = tree(parts)
    for n in range(count // 2):
        gains[n : n + 1, :] = join(total[2 * n : 2 * n + 1, :], swap(total[2 * n + 1 : 2 * n + 2, :]))
    for copy in copies:
        copy.wait()


def all_parts(value):
    size = lax.axis_size("tensor")
    others = [
        lax.ppermute(value, "tensor", [(i, (i + d) % size) for i in range(size)])
        for d in range(1, size)
    ]
    return [value] + others


def shards(features, gate_in, segments, gain, residue, rates, grad_out):
    _, length, width = features.shape
    group_count, mode_count = rates.shape
    count = lax.axis_size("ctx")
    full_width = width * lax.axis_size("tensor")
    size = lax.axis_size("dp")
    norm_factor = 1.0 / math.sqrt(size * length * count)
    tiles = width // LANES
    gain_table = gain.reshape(tiles, LANES)
    gain_row = gain.reshape(1, width)

    smem = pl.BlockSpec(memory_space=pltpu.SMEM)
    vmem = pl.BlockSpec(memory_space=pltpu.VMEM)
    hbm = pl.BlockSpec(memory_space=pl.ANY)
    here = pltpu.VMEM
    work = length * width * MODES
    wide = (length, width)
    scan_shape = here((length * tiles, LANES), f32)
    message = pltpu.HBM((count, MODES + EXTRA, LANES), f32)
    state_scratch = pltpu.VMEM((TILES * MODES, LANES), f32)

    def call(kernel, name, in_specs, out_specs, out_shape, scratch, flops):
        return pl.pallas_call(
            kernel,
            in_specs=in_specs,
            out_specs=out_specs,
            out_shape=out_shape,
            scratch_shapes=scratch,
            compiler_params=pltpu.CompilerParams(vmem_limit_bytes=16 * 1024 * 1024),
            cost_estimate=pl.CostEstimate(
                flops=flops // 10**6, bytes_accessed=1, transcendentals=0
            ),
            name=name,
        )

    def in_hbm(*values):
        return [pltpu.with_memory_space_constraint(value, pltpu.HBM) for value in values]

    raw = in_hbm(features[0], gate_in[0], grad_out[0], rates.T, residue.T, segments)
    dma = pltpu.SemaphoreType.DMA
    feats, grad_scan, squares, table, cuts = call(
        load_kernel,
        "load",
        [hbm] * 6,
        [vmem] * 4 + [smem],
        [
            here(wide, jnp.bfloat16),
            scan_shape,
            here((1, length), f32),
            here((2 * mode_count, tiles, LANES), f32),
            jax.ShapeDtypeStruct((COUNT,), jnp.int32),
        ],
        [
            pltpu.VMEM(wide, jnp.bfloat16),
            pltpu.VMEM(wide, jnp.bfloat16),
            pltpu.VMEM((mode_count, group_count), f32),
            pltpu.VMEM((mode_count, group_count), f32),
            pltpu.VMEM((1, length), jnp.int32),
            dma((3, COPIES)),
            dma((3,)),
        ],
        2 * length * width,
    )(*raw)
    squares = all_parts(squares)

    adjoint = call(
        adjoint_kernel,
        "adjoint",
        [smem, smem] + [vmem] * 2,
        vmem,
        here((tiles * MODES, LANES), f32),
        [],
        2 * work,
    )(segments, cuts, grad_scan, table)

    scan_scratch = pltpu.VMEM((length * TILES, LANES), f32)
    message_scratch = pltpu.VMEM(message.shape, f32)
    msg, inverse = call(
        lambda *refs: state_kernel(full_width, *refs),
        "states",
        [smem, smem] + [vmem] * 9,
        [hbm, vmem],
        [message, here((1, length), f32)],
        [message_scratch, scan_scratch, state_scratch, state_scratch, dma((HALVES,))],
        4 * work,
    )(segments, cuts, feats, grad_scan, *squares, table, gain_table, adjoint)

    def local(backward, cuts, *sources):
        return call(
            lambda *refs: local_kernel(backward, *refs),
            "local_backward" if backward else "local_forward",
            [smem, smem] + [vmem] * len(sources),
            hbm,
            pltpu.HBM(wide, f32),
            [scan_scratch, pltpu.VMEM(wide, f32), dma((HALVES,))]
            + ([] if backward else [scan_scratch]),
            4 * work,
        )(segments, cuts, *sources)

    conv_local = local(False, cuts, feats, table, inverse)
    msg = lax.all_to_all(msg, "ctx", 0, 0, tiled=True)
    late_cuts, msg, conv_local = lax.optimization_barrier((cuts, msg, conv_local))

    own = lax.axis_index("ctx").astype(jnp.int32).reshape(1)
    back = call(
        lambda *refs: carry_kernel(length, norm_factor, *refs),
        "carries",
        [smem] + [vmem] * 4,
        hbm,
        message,
        [message_scratch, pltpu.VMEM((count, MODES, LANES), f32), dma((COPIES,))],
        32 * count * MODES * LANES,
    )(own, msg, rates.T, residue.T, gain_row)

    grad_local = local(True, late_cuts, grad_scan, table)
    back = lax.all_to_all(back, "ctx", 0, 0, tiled=True)

    matmuls = 3 * 2 * length * width * WIDE
    scaled, inner, totals = call(
        backward_kernel,
        "backward",
        [smem, vmem, hbm, vmem, vmem],
        [vmem] * 3,
        [here(wide, f32), here((1, length), f32), here((count, LANES), f32)],
        [pltpu.VMEM((length, LANES), f32), pltpu.VMEM(wide, f32), dma((COPIES,))],
        matmuls,
    )(cuts, back, *in_hbm(grad_local), feats, gain_row)
    inner = all_parts(inner)
    other = lax.ppermute(totals, "dp", [(i, (i + 1) % size) for i in range(size)])

    mixed, grad_gate = call(
        forward_kernel,
        "forward",
        [smem] + [vmem] * 3 + [hbm, vmem],
        [hbm] * 2,
        [jax.ShapeDtypeStruct(wide, jnp.bfloat16)] * 2,
        [pltpu.VMEM(wide, f32)]
        + [pltpu.VMEM(wide, jnp.bfloat16)] * 3
        + [dma((2, COPIES)), dma((COPIES,))],
        matmuls,
    )(cuts, back, conv_local, gate_in[0], raw[2], gain_row)

    grad_features, grad_residue, grad_gain = call(
        lambda *refs: feature_kernel(full_width, *refs),
        "features",
        [vmem] * 9,
        [hbm, vmem, vmem],
        [
            jax.ShapeDtypeStruct(wide, jnp.bfloat16),
            jax.ShapeDtypeStruct((mode_count, group_count), f32),
            jax.ShapeDtypeStruct((tiles, LANES), f32),
        ],
        [pltpu.VMEM(wide, jnp.bfloat16), dma((COPIES,))],
        4 * length * width,
    )(scaled, feats, inverse, *inner, totals, other)
    return (
        mixed[None],
        grad_features[None],
        grad_gate[None],
        grad_residue.T,
        grad_gain.reshape(width),
    )


def solution(mesh):
    placed = (
        P("dp", "ctx", "tensor"),
        P("dp", "ctx", "tensor"),
        P("dp", "ctx"),
        P("tensor"),
        P("tensor", None),
        P("tensor", None),
        P("dp", "ctx", "tensor"),
    )
    return jax.shard_map(
        shards,
        mesh=mesh,
        in_specs=placed,
        out_specs=(
            P("dp", "ctx", "tensor"),
            P("dp", "ctx", "tensor"),
            P("dp", "ctx", "tensor"),
            P("tensor", None),
            P("tensor"),
        ),
        check_vma=False,
    )
```

```python
import math

import jax
import jax.numpy as jnp
from jax import lax
from jax.experimental import pallas as pl
from jax.experimental.pallas import tpu as pltpu
from jax.sharding import PartitionSpec as P

epsilon = 1e-06
LANES = 128
TILES = 8
HALVES = 2
MODES = 16
GROUP = 16
UNROLL = 16
COUNT = 4
COPIES = 2
BLOCKS = 8
WIDE = 2 * LANES
ROWS = MODES + 2
HIGHEST = lax.Precision.HIGHEST
f32 = jnp.float32


def lane_iota(rows):
    return lax.broadcasted_iota(jnp.int32, (rows, LANES), 1)


def swap(value):
    return pltpu.roll(value, LANES // 2, axis=1)


def join(low, high):
    return jnp.where(lane_iota(low.shape[0]) < LANES // 2, low, high)


def total_row(parts):
    return tree([part[...] for part in parts])


def inverse_of(parts, full_width):
    return lax.rsqrt(total_row(parts) / full_width + epsilon)


def column(row):
    length = row.shape[1]
    row = jnp.broadcast_to(row, (8, length))
    return jnp.broadcast_to(jnp.transpose(row)[:, 0:1], (length, LANES))


def block_ones():
    left = lax.broadcasted_iota(jnp.int32, (LANES, LANES), 0) // GROUP
    right = lax.broadcasted_iota(jnp.int32, (LANES, LANES), 1) // GROUP
    return jnp.where(left == right, 1.0, 0.0).astype(jnp.bfloat16)


def exact_dot(value, ones):
    high = value.astype(jnp.bfloat16).astype(f32)
    middle = (value - high).astype(jnp.bfloat16).astype(f32)
    parts = jnp.concatenate([high, middle, value - high - middle], axis=0)
    full = jnp.dot(parts.astype(jnp.bfloat16), ones, preferred_element_type=f32)
    rows = value.shape[0]
    return full[0:rows] + (full[rows : 2 * rows] + full[2 * rows :])


def lanes_of(half, tile):
    return pl.ds(pl.multiple_of((half * TILES + tile) * LANES, LANES), LANES)


def tile_of(ref, half, tile):
    return ref[:, lanes_of(half, tile)].astype(f32)


def scan_rows(half, tile, length):
    return pl.ds(half * length * TILES + tile, length, stride=TILES)


def table_of(table, half, first):
    at = pl.ds(pl.multiple_of(half * TILES, TILES), TILES)
    return [table[first + r, at, :] for r in range(MODES)]


def decay_of(table, half):
    return [jnp.exp(-rate) for rate in table_of(table, half, 0)]


def weight_of(table, half):
    return table_of(table, half, MODES)


def state_rows(half, r):
    return pl.ds(half * TILES * MODES + r, TILES, stride=MODES)


def tree(values):
    values = list(values)
    while len(values) > 1:
        values = [a + b for a, b in zip(values[::2], values[1::2])]
    return values[0]


def scan(length, seg, cuts, step, carry, backward):
    groups = length // UNROLL

    def run(group, carry, masked):
        base = group * UNROLL
        for u in range(UNROLL):
            t = base + (UNROLL - 1 - u if backward else u)
            keep = None
            if masked:
                near = jnp.minimum(t + 1, length - 1) if backward else jnp.maximum(t - 1, 0)
                keep = seg[0, t] == seg[0, near]
            carry = step(t, carry, keep)
        return carry

    def stretch(p, carry):
        now, states = carry
        if backward:
            cut = jnp.where(p < COUNT - 1, cuts[jnp.maximum(COUNT - 2 - p, 0)], 0)
            group = (cut - 1) // UNROLL
            stop = jnp.where(
                cut >= length, now, jnp.where(cut <= 0, 0, jnp.minimum(now, group + 1))
            )
            states = lax.fori_loop(
                0, now - stop, lambda i, value: run(now - 1 - i, value, False), states
            )
            broken = (cut > 0) & (cut < length) & (group < now)
            after = group
        else:
            cut = jnp.where(p < COUNT - 1, cuts[jnp.minimum(p, COUNT - 2)], length)
            group = cut // UNROLL
            stop = jnp.where(
                cut <= 0, now, jnp.where(cut >= length, groups, jnp.maximum(now, group))
            )
            states = lax.fori_loop(now, stop, lambda i, value: run(i, value, False), states)
            broken = (cut > 0) & (cut < length) & (group >= now)
            after = group + 1
        states = lax.cond(
            broken, lambda value: run(group, value, True), lambda value: value, states
        )
        return jnp.where(broken, after, stop), states

    start = jnp.int32(groups if backward else 0)
    return lax.fori_loop(0, COUNT, stretch, (start, carry))[1]


def decayed(decay, state, keep):
    state = decay * state
    return state if keep is None else jnp.where(keep, state, 0.0)


def row_at(ref, half, length, t):
    return ref[pl.ds(pl.multiple_of((half * length + t) * TILES, TILES), TILES), :]


def lane_sums(value):
    return lax.dot_general(
        jnp.ones((8, LANES), f32),
        value,
        (((1,), (1,)), ((), ())),
        precision=HIGHEST,
        preferred_element_type=f32,
    )[0:1]


def load_kernel(
    feats_in, gate_in, grad_in, rates_in, residue_in, seg_in,
    feats, grad_scan, squares, table, cuts,
    gate, grad, rates, residue, seg, sems, small_sems,
):
    length, width = feats.shape
    small = [
        pltpu.make_async_copy(src, dst, small_sems.at[n])
        for n, (src, dst) in enumerate(((rates_in, rates), (residue_in, residue), (seg_in, seg)))
    ]
    for copy in small:
        copy.start()
    feat_copies = row_copies(feats_in, feats, sems.at[0])
    copies = row_copies(gate_in, gate, sems.at[1]) + row_copies(grad_in, grad, sems.at[2])
    for copy in small:
        copy.wait()
    expand(rates, residue, seg, table, cuts)
    wait_all(feat_copies)
    partial = jnp.zeros((length, LANES), f32)
    for tile in range(width // LANES):
        value = tile_of(feats, 0, tile)
        partial = partial + value * value
    squares[...] = lane_sums(partial)
    wait_all(copies)
    for half in range(HALVES):
        for tile in range(TILES):
            value = tile_of(gate, half, tile) * tile_of(grad, half, tile)
            grad_scan[scan_rows(half, tile, length), :] = value


def mode_params(rates, residue):
    rate = rates[...]
    twice = 2.0 * rate
    series = 1.0 - twice / 6.0
    for n in (5, 4, 3, 2):
        series = 1.0 - twice / n * series
    root = jnp.sqrt(jnp.where(twice < 0.25, twice * series, 1.0 - jnp.exp(-twice)))
    return jnp.concatenate([rate, residue[...] * root, root], axis=0)


def spread_groups(packed, width, first):
    group_count = packed.shape[1]
    group = lax.broadcasted_iota(jnp.int32, (group_count, width), 0)
    lane = lax.broadcasted_iota(jnp.int32, (group_count, width), 1)
    spread = jnp.where(first(lane) == group, 1.0, 0.0).astype(jnp.bfloat16)
    return exact_dot(packed, spread)


def own_mode(value):
    row = lax.broadcasted_iota(jnp.int32, value.shape, 0)
    lane = lax.broadcasted_iota(jnp.int32, value.shape, 1)
    return jnp.sum(jnp.where(row == lane % GROUP, value, 0.0), axis=0, keepdims=True)


def expand(rates, residue, seg, table, cuts):
    width = table.shape[1] * LANES
    full = spread_groups(mode_params(rates, residue), width, lambda lane: lane // GROUP)
    for tile in range(width // LANES):
        at = slice(tile * LANES, (tile + 1) * LANES)
        table[:, tile, :] = full[0 : 2 * MODES, at]
    for p in range(COUNT - 1):
        cuts[p] = jnp.sum(jnp.where(seg[...] <= p, 1, 0))
    cuts[COUNT - 1] = seg.shape[1]


def adjoint_kernel(seg, cuts, grad_scan, table, adj):
    length = seg.shape[1]

    def run(half, _):
        decay = decay_of(table, half)

        def step(t, states, keep):
            value = row_at(grad_scan, half, length, t)
            return tuple(decayed(decay[r], states[r], keep) + value for r in range(MODES))

        zero = jnp.zeros((TILES, LANES), f32)
        states = scan(length, seg, cuts, step, (zero,) * MODES, True)
        for r in range(MODES):
            adj[state_rows(half, r), :] = states[r]
        return _

    lax.fori_loop(0, HALVES, run, 0)


def state_kernel(
    full_width, seg, cuts, feats, grad_scan, part0, part1, part2, part3, table, gain, adj,
    msg_out, inverse, grad_out, msg, feat_scan, ends, sums, sems, grad_sems,
):
    length = feats.shape[0]
    grad_copies = row_copies(grad_scan, grad_out, grad_sems)
    inverse[...] = inverse_of((part0, part1, part2, part3), full_width)
    scale = column(inverse[...])
    share = msg.shape[0] // HALVES

    def send(half):
        at = pl.ds(half * share, share)
        return pltpu.make_async_copy(msg.at[at, :], msg_out.at[at, :], sems.at[half])

    for half in range(HALVES):
        state_half(
            length, half, scale, seg, cuts, feats, grad_scan, table, gain, adj,
            msg, feat_scan, ends, sums,
        )
        send(half).start()
    for half in range(HALVES):
        send(half).wait()
    wait_all(grad_copies)


def state_half(
    length, half, scale, seg, cuts, feats, grad_scan, table, gain, adj,
    msg, feat_scan, ends, sums,
):
    for tile in range(TILES):
        feat_scan[scan_rows(0, tile, length), :] = tile_of(feats, half, tile) * scale
    decay = decay_of(table, half)

    def step(t, carry, keep):
        value = row_at(feat_scan, 0, length, t)
        grads = row_at(grad_scan, half, length, t)
        states = [decayed(decay[r], carry[r], keep) + value for r in range(MODES)]
        totals = [carry[MODES + r] + grads * states[r] for r in range(MODES)]
        return tuple(states) + tuple(totals)

    zero = jnp.zeros((TILES, LANES), f32)
    carry = scan(length, seg, cuts, step, (zero,) * (2 * MODES), False)
    gains = gain[pl.ds(pl.multiple_of(half * TILES, TILES), TILES), :]
    weights = weight_of(table, half)
    for r in range(MODES):
        ends[pl.ds(r, TILES, stride=MODES), :] = carry[r]
        sums[r * TILES : (r + 1) * TILES, :] = carry[MODES + r] * gains
    gain_row = tree([weights[r] * carry[MODES + r] for r in range(MODES)])
    spread = exact_dot(sums[...], block_ones())
    lane_mode = lane_iota(TILES) % GROUP
    mode_row = tree(
        [
            jnp.where(lane_mode == r, spread[r * TILES : (r + 1) * TILES, :], 0.0)
            for r in range(MODES)
        ]
    )
    even = join(gain_row, swap(mode_row))
    odd = join(swap(gain_row), mode_row)
    first = jnp.full((1, LANES), seg[0, 0], jnp.int32).astype(f32)
    last = jnp.full((1, LANES), seg[0, length - 1], jnp.int32).astype(f32)
    near = join(first, last)

    for tile in range(TILES):
        state = ends[tile * MODES : (tile + 1) * MODES, :]
        own = (half * TILES + tile) * MODES
        adjoint = adj[pl.ds(pl.multiple_of(own, MODES), MODES), :]
        at = 2 * (half * TILES + tile) * ROWS
        msg[at : at + MODES, :] = join(state, swap(adjoint))
        msg[at + MODES : at + MODES + 1, :] = even[tile : tile + 1, :]
        msg[at + MODES + 1 : at + ROWS, :] = near
        at += ROWS
        msg[at : at + MODES, :] = join(swap(state), adjoint)
        msg[at + MODES : at + MODES + 1, :] = odd[tile : tile + 1, :]
        msg[at + MODES + 1 : at + ROWS, :] = near


def carry_kernel(
    span, norm_factor, own, msg, rates, residue, gain, out_hbm, out, carries, sems
):
    count = msg.shape[0] // ROWS
    share = rates.shape[1] // count
    first = own[0] * share
    full = spread_groups(
        mode_params(rates, residue), LANES, lambda lane: first + lane % (LANES // 2) // GROUP
    )
    rate, weight = full[0:MODES], full[MODES : 2 * MODES]
    root = own_mode(full[2 * MODES :])
    at = pl.ds(pl.multiple_of(own[0] // 2 * LANES, LANES), LANES)
    gains = gain[:, at]
    odd = own[0] % 2 == 1
    gains = jnp.where(odd, join(swap(gains), gains), join(gains, swap(gains)))
    single = jnp.exp(-rate)
    whole = jnp.exp(-rate * float(span))
    state = jnp.zeros((MODES, LANES), f32)
    before = None
    ends = [msg[i * ROWS : i * ROWS + MODES, :] for i in range(count)]
    ids = [msg[i * ROWS + MODES + 1 : (i + 1) * ROWS, :] for i in range(count)]
    for m in range(count):
        other = count - 1 - m
        fresh = join(ends[m], ends[other])
        near = join(ids[m], ids[other])
        far = join(swap(ids[m]), swap(ids[other]))
        if before is None:
            carries[m] = state
            state = fresh
        else:
            carries[m] = jnp.where(near == before, state, 0.0)
            state = fresh + jnp.where(far == before, whole * state, 0.0)
        before = far
    total = jnp.zeros((MODES, LANES), f32)
    row = jnp.zeros((1, LANES), f32)
    for i in range(count):
        carried = join(carries[i], carries[count - 1 - i])
        out[i * ROWS : i * ROWS + MODES, :] = carried
        total = total + carried * swap(ends[i])
        row = row + msg[i * ROWS + MODES : i * ROWS + MODES + 1, :]
    total = total * single
    gain_row = jnp.sum(weight * total, axis=0, keepdims=True)
    spread = exact_dot(total * gains, block_ones())
    pick = lane_iota(MODES) % GROUP == lax.broadcasted_iota(jnp.int32, (MODES, LANES), 0)
    mode_row = jnp.sum(jnp.where(pick, spread, 0.0), axis=0, keepdims=True)
    row = (row + join(gain_row, swap(mode_row))) * join(jnp.ones((1, LANES), f32), root)
    row = row * norm_factor
    modes = join(own_mode(rate), own_mode(weight))
    for i in range(count):
        out[i * ROWS + MODES : i * ROWS + MODES + 1, :] = row
        out[i * ROWS + MODES + 1 : (i + 1) * ROWS, :] = modes
    copies = []
    part = out.shape[0] // COPIES
    for i in range(COPIES):
        at = pl.ds(i * part, part)
        copies.append(pltpu.make_async_copy(out.at[at, :], out_hbm.at[at, :], sems.at[i]))
        copies[-1].start()
    for copy in copies:
        copy.wait()


def local_kernel(backward, seg, cuts, table_in, *refs):
    if backward:
        grad_in, feats_in, gain, out, inner, feats, result, feat_sems, *rest = refs
        value_out, sems, partial, grad_scan, grad_sems, table, table_sem = rest
        table_copy = pltpu.make_async_copy(table_in, table, table_sem.at[0])
        table_copy.start()
        grad_copies = row_copies(grad_in, grad_scan, grad_sems)
    else:
        feats_in, inverse, value_out, table_out, result, feat_sems, scan_in, feats, table_sem = refs
        table = table_in
        table_copy = pltpu.make_async_copy(table, table_out, table_sem.at[0])
        table_copy.start()
    length = seg.shape[1]
    feat_copies = row_copies(feats_in, feats, feat_sems)
    if not backward:
        scale = column(inverse[...])
        wait_all(feat_copies)
    copies = []
    for half in range(HALVES):
        if backward:
            values, at_half = grad_scan, half
            part = COPIES // HALVES
            wait_all(grad_copies[half * part : (half + 1) * part])
            if half == 0:
                table_copy.wait()
        else:
            values, at_half = scan_in, 0
            for tile in range(TILES):
                values[scan_rows(0, tile, length), :] = tile_of(feats, half, tile) * scale
        decay = decay_of(table, half)
        weight = weight_of(table, half)

        def step(t, states, keep):
            value = row_at(values, at_half, length, t)
            states = tuple(decayed(decay[r], states[r], keep) + value for r in range(MODES))
            result[pl.ds(pl.multiple_of(t * TILES, TILES), TILES), :] = tree(
                [weight[r] * states[r] for r in range(MODES)]
            )
            return states

        zero = jnp.zeros((TILES, LANES), f32)
        scan(length, seg, cuts, step, (zero,) * MODES, backward)
        for tile in range(TILES):
            value_out[:, lanes_of(half, tile)] = result[pl.ds(tile, length, stride=TILES), :]
        if backward:
            at = pl.ds(half * TILES * LANES, TILES * LANES)
            copies.append(pltpu.make_async_copy(value_out.at[:, at], out.at[:, at], sems.at[half]))
            copies[-1].start()
    if backward:
        wait_all(feat_copies)
        inner[...] = inner_sums(value_out, feats, gain, partial)
    else:
        table_copy.wait()
    wait_all(copies)


def inner_sums(value, feats, gain, partial):
    length, width = feats.shape
    step = length // BLOCKS
    for i in range(BLOCKS):
        here = slice(i * step, (i + 1) * step)
        partial[here, :] = tree(
            [
                value[here, at] * gain[:, at] * feats[here, at].astype(f32)
                for at in tiles_at(width)
            ]
        )
    return lane_sums(partial[...])


def from_owners(back, pair, rows, upper):
    parts = []
    for n in range(2):
        first = (4 * pair + 2 * n) * ROWS
        low = back[first + rows.start : first + rows.stop, :]
        high = back[first + ROWS + rows.start : first + ROWS + rows.stop, :]
        parts.append(join(swap(low), high) if upper else join(low, swap(high)))
    return jnp.concatenate(parts, axis=1)


def powers(cuts, back, pair, length, ahead):
    t = lax.broadcasted_iota(jnp.int32, (length, WIDE), 0)
    modes = slice(MODES + 1, MODES + 2)
    rate = from_owners(back, pair, modes, False)
    weight = from_owners(back, pair, modes, True)
    sub = lax.broadcasted_iota(jnp.int32, (8, WIDE), 0).astype(f32)
    further = jnp.exp(-8.0 * rate)
    if ahead:
        edge = jnp.int32(0)
        for p in range(COUNT - 1):
            edge = jnp.maximum(edge, jnp.where(cuts[p] < length, cuts[p], 0))
        linked = t >= edge
        lag = 8.0 - sub
    else:
        edge = jnp.int32(length)
        for p in range(COUNT - 1):
            edge = jnp.minimum(edge, jnp.where(cuts[p] > 0, cuts[p], length))
        linked = t < edge
        lag = sub + 1.0
    blocks = [jnp.exp(-lag * rate) * weight]
    for _ in range(length // 8 - 1):
        blocks.append(blocks[-1] * further)
    power = jnp.concatenate(blocks[::-1] if ahead else blocks, axis=0)
    return split(jnp.where(linked, power, 0.0))


def split(value):
    high = value.astype(jnp.bfloat16)
    return high, (value - high.astype(f32)).astype(jnp.bfloat16)


def from_carry(cuts, back, pair, length, ahead):
    carry = from_owners(back, pair, slice(0, MODES), ahead)
    own = lax.broadcasted_iota(jnp.int32, (WIDE, WIDE), 0) // MODES == (
        lax.broadcasted_iota(jnp.int32, (WIDE, WIDE), 1) // GROUP
    )

    def spread(value):
        value = jnp.concatenate([value.astype(f32)] * (WIDE // MODES), axis=0)
        return jnp.where(own, value, 0.0).astype(jnp.bfloat16)

    high, low = (spread(value) for value in split(carry))
    near, far = powers(cuts, back, pair, length, ahead)
    dot = lambda x, y: jnp.dot(x, y, preferred_element_type=f32)
    return dot(near, high) + (dot(far, high) + dot(near, low))


def row_copy(src, dst, sems, part, parts=COPIES):
    step = dst.shape[0] // parts
    at = pl.ds(part * step, step)
    return pltpu.make_async_copy(src.at[at, :], dst.at[at, :], sems.at[part])


def row_copies(src, dst, sems, parts=COPIES):
    copies = [row_copy(src, dst, sems, part, parts) for part in range(parts)]
    for copy in copies:
        copy.start()
    return copies


def wait_all(copies):
    for copy in copies:
        copy.wait()


def tiles_at(width):
    return [slice(tile * LANES, (tile + 1) * LANES) for tile in range(width // LANES)]


def backward_kernel(
    cuts, back, inner_local, feats, gain, gate_in, grad_in,
    carried, inner, totals, gate, grad, partial, sems,
):
    length, width = feats.shape
    copies = []
    for n, (src, dst) in enumerate(((gate_in, gate), (grad_in, grad))):
        copies += row_copies(src, dst, sems.at[n], 1)
    for n in range(totals.shape[0]):
        totals[n : n + 1, :] = back[n * ROWS + MODES : n * ROWS + MODES + 1, :]
    for pair in range(width // WIDE):
        at = slice(pair * WIDE, (pair + 1) * WIDE)
        carried[:, at] = from_carry(cuts, back, pair, length, True)
    inner[...] = inner_local[...] + inner_sums(carried, feats, gain, partial)
    wait_all(copies)


def forward_kernel(
    cuts, back, local, gate, grad, gain, mixed, grad_gate, carried, mixed_v, grad_gate_v, sems
):
    length, width = gate.shape
    for pair in range(width // WIDE):
        at = slice(pair * WIDE, (pair + 1) * WIDE)
        carried[:, at] = from_carry(cuts, back, pair, length, False)
    copies = []
    step = length // BLOCKS
    for i in range(BLOCKS):
        here = slice(i * step, (i + 1) * step)
        for at in tiles_at(width):
            conv = (local[here, at] + carried[here, at]) * gain[:, at]
            mixed_v[here, at] = (gate[here, at].astype(f32) * conv).astype(jnp.bfloat16)
            grad_gate_v[here, at] = (grad[here, at].astype(f32) * conv).astype(jnp.bfloat16)
        if (i + 1) % (BLOCKS // COPIES) == 0:
            part = (i + 1) // (BLOCKS // COPIES) - 1
            for n, (src, dst) in enumerate(((mixed_v, mixed), (grad_gate_v, grad_gate))):
                copies.append(row_copy(src, dst, sems.at[n], part))
                copies[-1].start()
    wait_all(copies)


def feature_kernel(
    full_width, local, carried, feats, gain, inverse, i0, i1, i2, i3, own, other,
    out, modes, gains, out_v, sems,
):
    length, width = feats.shape
    scale = column(inverse[...])
    factor = column(total_row((i0, i1, i2, i3))) * scale * scale / full_width
    copies = []
    step = length // BLOCKS
    for i in range(BLOCKS):
        here = slice(i * step, (i + 1) * step)
        for at in tiles_at(width):
            scaled = (local[here, at] + carried[here, at]) * gain[:, at]
            value = scale[here] * (scaled - feats[here, at].astype(f32) * factor[here])
            out_v[here, at] = value.astype(jnp.bfloat16)
        if (i + 1) % (BLOCKS // COPIES) == 0:
            copies.append(row_copy(out_v, out, sems, (i + 1) // (BLOCKS // COPIES) - 1))
            copies[-1].start()

    total = own[...] + other[...]
    count = total.shape[0]
    groups = modes.shape[1]
    share = groups // count
    slot = lax.broadcasted_iota(jnp.int32, (count, groups), 1) // share
    pick = jnp.where(slot == lax.broadcasted_iota(jnp.int32, (count, groups), 0), 1.0, 0.0)
    spread = lax.dot_general(
        total,
        pick.astype(f32),
        (((0,), (0,)), ((), ())),
        precision=HIGHEST,
        preferred_element_type=f32,
    )
    member = lax.broadcasted_iota(jnp.int32, (MODES, groups), 1) % share
    parts = [
        jnp.where(member == n, spread[LANES // 2 + n * MODES : LANES // 2 + (n + 1) * MODES], 0.0)
        for n in range(share)
    ]
    modes[...] = tree(parts)
    for n in range(count // 2):
        gains[n : n + 1, :] = join(total[2 * n : 2 * n + 1, :], swap(total[2 * n + 1 : 2 * n + 2, :]))
    for copy in copies:
        copy.wait()


def all_parts(value):
    size = lax.axis_size("tensor")
    others = [
        lax.ppermute(value, "tensor", [(i, (i + d) % size) for i in range(size)])
        for d in range(1, size)
    ]
    return [value] + others


def shards(features, gate_in, segments, gain, residue, rates, grad_out):
    _, length, width = features.shape
    group_count, mode_count = rates.shape
    count = lax.axis_size("ctx")
    full_width = width * lax.axis_size("tensor")
    size = lax.axis_size("dp")
    norm_factor = 1.0 / math.sqrt(size * length * count)
    tiles = width // LANES
    gain_table = gain.reshape(tiles, LANES)
    gain_row = gain.reshape(1, width)

    smem = pl.BlockSpec(memory_space=pltpu.SMEM)
    vmem = pl.BlockSpec(memory_space=pltpu.VMEM)
    hbm = pl.BlockSpec(memory_space=pl.ANY)
    here = pltpu.VMEM
    work = length * width * MODES
    wide = (length, width)
    scan_shape = here((length * tiles, LANES), f32)
    message = pltpu.HBM((count * ROWS, LANES), f32)

    def exchange(value):
        value = value.reshape(count, 1, ROWS * LANES)
        return lax.all_to_all(value, "ctx", 0, 0, tiled=True).reshape(message.shape)

    state_scratch = pltpu.VMEM((TILES * MODES, LANES), f32)

    def call(kernel, name, in_specs, out_specs, out_shape, scratch, flops):
        return pl.pallas_call(
            kernel,
            in_specs=in_specs,
            out_specs=out_specs,
            out_shape=out_shape,
            scratch_shapes=scratch,
            compiler_params=pltpu.CompilerParams(vmem_limit_bytes=16 * 1024 * 1024),
            cost_estimate=pl.CostEstimate(
                flops=flops // 10**6, bytes_accessed=1, transcendentals=0
            ),
            name=name,
        )

    def in_hbm(*values):
        return [pltpu.with_memory_space_constraint(value, pltpu.HBM) for value in values]

    raw = in_hbm(features[0], gate_in[0], grad_out[0], rates.T, residue.T, segments)
    dma = pltpu.SemaphoreType.DMA
    feats, grad_scan, squares, table, cuts = call(
        load_kernel,
        "load",
        [hbm] * 6,
        [vmem] * 4 + [smem],
        [
            here(wide, jnp.bfloat16),
            scan_shape,
            here((1, length), f32),
            here((2 * mode_count, tiles, LANES), f32),
            jax.ShapeDtypeStruct((COUNT,), jnp.int32),
        ],
        [
            pltpu.VMEM(wide, jnp.bfloat16),
            pltpu.VMEM(wide, jnp.bfloat16),
            pltpu.VMEM((mode_count, group_count), f32),
            pltpu.VMEM((mode_count, group_count), f32),
            pltpu.VMEM((1, length), jnp.int32),
            dma((3, COPIES)),
            dma((3,)),
        ],
        2 * length * width,
    )(*raw)
    squares = all_parts(squares)

    adjoint = call(
        adjoint_kernel,
        "adjoint",
        [smem, smem] + [vmem] * 2,
        vmem,
        here((tiles * MODES, LANES), f32),
        [],
        2 * work,
    )(segments, cuts, grad_scan, table)

    scan_scratch = pltpu.VMEM((length * TILES, LANES), f32)
    message_scratch = pltpu.VMEM(message.shape, f32)
    msg, inverse, late_grad = call(
        lambda *refs: state_kernel(full_width, *refs),
        "states",
        [smem, smem] + [vmem] * 9,
        [hbm, vmem, hbm],
        [message, here((1, length), f32), pltpu.HBM((length * tiles, LANES), f32)],
        [
            message_scratch,
            scan_scratch,
            state_scratch,
            state_scratch,
            dma((HALVES,)),
            dma((COPIES,)),
        ],
        4 * work,
    )(segments, cuts, feats, grad_scan, *squares, table, gain_table, adjoint)

    def local(backward, cuts, *sources):
        return call(
            lambda *refs: local_kernel(backward, *refs),
            "local_backward" if backward else "local_forward",
            [smem, smem] + ([hbm, hbm, hbm, vmem] if backward else [vmem, hbm, vmem]),
            [hbm, vmem, vmem] if backward else [vmem, hbm],
            [pltpu.HBM(wide, f32), here((1, length), f32), here(wide, jnp.bfloat16)]
            if backward
            else [here(wide, f32), pltpu.HBM(table.shape, f32)],
            [scan_scratch, dma((COPIES,))]
            + (
                [
                    pltpu.VMEM(wide, f32),
                    dma((HALVES,)),
                    pltpu.VMEM((length, LANES), f32),
                    pltpu.VMEM((length * tiles, LANES), f32),
                    dma((COPIES,)),
                    pltpu.VMEM(table.shape, f32),
                    dma((1,)),
                ]
                if backward
                else [scan_scratch, pltpu.VMEM(wide, jnp.bfloat16), dma((1,))]
            ),
            4 * work,
        )(segments, cuts, *sources)

    conv_local, late_table = local(False, cuts, table, raw[0], inverse)
    msg = exchange(msg)
    late_cuts, msg, conv_local = lax.optimization_barrier((cuts, msg, conv_local))

    own = lax.axis_index("ctx").astype(jnp.int32).reshape(1)
    back = call(
        lambda *refs: carry_kernel(length, norm_factor, *refs),
        "carries",
        [smem] + [vmem] * 4,
        hbm,
        message,
        [message_scratch, pltpu.VMEM((count, MODES, LANES), f32), dma((COPIES,))],
        32 * count * MODES * LANES,
    )(own, msg, rates.T, residue.T, gain_row)

    grad_local, inner_local, feats = local(
        True, late_cuts, *in_hbm(late_table, late_grad), raw[0], gain_row
    )
    back = exchange(back)

    matmuls = 3 * 2 * length * width * WIDE
    carried, inner, totals, gate, grad = call(
        backward_kernel,
        "backward",
        [smem] + [vmem] * 4 + [hbm] * 2,
        [vmem] * 5,
        [
            here(wide, f32),
            here((1, length), f32),
            here((count, LANES), f32),
            here(wide, jnp.bfloat16),
            here(wide, jnp.bfloat16),
        ],
        [pltpu.VMEM((length, LANES), f32), dma((2, COPIES))],
        matmuls,
    )(cuts, back, inner_local, feats, gain_row, raw[1], raw[2])
    inner = all_parts(inner)
    other = lax.ppermute(totals, "dp", [(i, (i + 1) % size) for i in range(size)])

    mixed, grad_gate = call(
        forward_kernel,
        "forward",
        [smem] + [vmem] * 5,
        [hbm] * 2,
        [jax.ShapeDtypeStruct(wide, jnp.bfloat16)] * 2,
        [pltpu.VMEM(wide, f32)]
        + [pltpu.VMEM(wide, jnp.bfloat16)] * 2
        + [dma((2, COPIES))],
        matmuls,
    )(cuts, back, conv_local, gate, grad, gain_row)

    grad_features, grad_residue, grad_gain = call(
        lambda *refs: feature_kernel(full_width, *refs),
        "features",
        [vmem] * 11,
        [hbm, vmem, vmem],
        [
            jax.ShapeDtypeStruct(wide, jnp.bfloat16),
            jax.ShapeDtypeStruct((mode_count, group_count), f32),
            jax.ShapeDtypeStruct((tiles, LANES), f32),
        ],
        [pltpu.VMEM(wide, jnp.bfloat16), dma((COPIES,))],
        4 * length * width,
    )(grad_local, carried, feats, gain_row, inverse, *inner, totals, other)
    return (
        mixed[None],
        grad_features[None],
        grad_gate[None],
        grad_residue.T,
        grad_gain.reshape(width),
    )


def solution(mesh):
    placed = (
        P("dp", "ctx", "tensor"),
        P("dp", "ctx", "tensor"),
        P("dp", "ctx"),
        P("tensor"),
        P("tensor", None),
        P("tensor", None),
        P("dp", "ctx", "tensor"),
    )
    return jax.shard_map(
        shards,
        mesh=mesh,
        in_specs=placed,
        out_specs=(
            P("dp", "ctx", "tensor"),
            P("dp", "ctx", "tensor"),
            P("dp", "ctx", "tensor"),
            P("tensor", None),
            P("tensor"),
        ),
        check_vma=False,
    )
```

```python
import math

import jax
import jax.numpy as jnp
from jax import lax
from jax.experimental import pallas as pl
from jax.experimental.pallas import tpu as pltpu
from jax.sharding import PartitionSpec as P

epsilon = 1e-06
LANES = 128
TILES = 8
HALVES = 2
MODES = 16
GROUP = 16
UNROLL = 16
COUNT = 4
COPIES = 2
BLOCKS = 8
WIDE = 2 * LANES
ROWS = MODES + 2
HIGHEST = lax.Precision.HIGHEST
f32 = jnp.float32


def lane_iota(rows):
    return lax.broadcasted_iota(jnp.int32, (rows, LANES), 1)


def swap(value):
    return pltpu.roll(value, LANES // 2, axis=1)


def join(low, high):
    return jnp.where(lane_iota(low.shape[0]) < LANES // 2, low, high)


def total_row(parts):
    return tree([part[...] for part in parts])


def inverse_of(parts, full_width):
    return lax.rsqrt(total_row(parts) / full_width + epsilon)


def column(row):
    length = row.shape[1]
    row = jnp.broadcast_to(row, (8, length))
    return jnp.broadcast_to(jnp.transpose(row)[:, 0:1], (length, LANES))


def block_ones():
    left = lax.broadcasted_iota(jnp.int32, (LANES, LANES), 0) // GROUP
    right = lax.broadcasted_iota(jnp.int32, (LANES, LANES), 1) // GROUP
    return jnp.where(left == right, 1.0, 0.0).astype(jnp.bfloat16)


def exact_dot(value, ones):
    high = value.astype(jnp.bfloat16).astype(f32)
    middle = (value - high).astype(jnp.bfloat16).astype(f32)
    parts = jnp.concatenate([high, middle, value - high - middle], axis=0)
    full = jnp.dot(parts.astype(jnp.bfloat16), ones, preferred_element_type=f32)
    rows = value.shape[0]
    return full[0:rows] + (full[rows : 2 * rows] + full[2 * rows :])


def lanes_of(half, tile):
    return pl.ds(pl.multiple_of((half * TILES + tile) * LANES, LANES), LANES)


def tile_of(ref, half, tile):
    return ref[:, lanes_of(half, tile)].astype(f32)


def scan_rows(half, tile, length):
    return pl.ds(half * length * TILES + tile, length, stride=TILES)


def table_of(table, half, first):
    at = pl.ds(pl.multiple_of(half * TILES, TILES), TILES)
    return [table[first + r, at, :] for r in range(MODES)]


def decay_of(table, half):
    return [jnp.exp(-rate) for rate in table_of(table, half, 0)]


def weight_of(table, half):
    return table_of(table, half, MODES)


def state_rows(half, r):
    return pl.ds(half * TILES * MODES + r, TILES, stride=MODES)


def tree(values):
    values = list(values)
    while len(values) > 1:
        values = [a + b for a, b in zip(values[::2], values[1::2])]
    return values[0]


def scan(length, seg, cuts, step, carry, backward):
    groups = length // UNROLL

    def run(group, carry, masked):
        base = group * UNROLL
        for u in range(UNROLL):
            t = base + (UNROLL - 1 - u if backward else u)
            keep = None
            if masked:
                near = jnp.minimum(t + 1, length - 1) if backward else jnp.maximum(t - 1, 0)
                keep = seg[0, t] == seg[0, near]
            carry = step(t, carry, keep)
        return carry

    def stretch(p, carry):
        now, states = carry
        if backward:
            cut = jnp.where(p < COUNT - 1, cuts[jnp.maximum(COUNT - 2 - p, 0)], 0)
            group = (cut - 1) // UNROLL
            stop = jnp.where(
                cut >= length, now, jnp.where(cut <= 0, 0, jnp.minimum(now, group + 1))
            )
            states = lax.fori_loop(
                0, now - stop, lambda i, value: run(now - 1 - i, value, False), states
            )
            broken = (cut > 0) & (cut < length) & (group < now)
            after = group
        else:
            cut = jnp.where(p < COUNT - 1, cuts[jnp.minimum(p, COUNT - 2)], length)
            group = cut // UNROLL
            stop = jnp.where(
                cut <= 0, now, jnp.where(cut >= length, groups, jnp.maximum(now, group))
            )
            states = lax.fori_loop(now, stop, lambda i, value: run(i, value, False), states)
            broken = (cut > 0) & (cut < length) & (group >= now)
            after = group + 1
        states = lax.cond(
            broken, lambda value: run(group, value, True), lambda value: value, states
        )
        return jnp.where(broken, after, stop), states

    def general(carry):
        start = jnp.int32(groups if backward else 0)
        return lax.fori_loop(0, COUNT, stretch, (start, carry))[1]

    def unbroken(carry):
        def body(i, carry):
            return run(groups - 1 - i if backward else i, carry, False)

        return lax.fori_loop(0, groups, body, carry)

    broken = cuts[0] < 0
    for p in range(COUNT - 1):
        broken = broken | ((cuts[p] > 0) & (cuts[p] < length))
    return lax.cond(broken, general, unbroken, carry)


def decayed(decay, state, keep):
    state = decay * state
    return state if keep is None else jnp.where(keep, state, 0.0)


def row_at(ref, half, length, t):
    return ref[pl.ds(pl.multiple_of((half * length + t) * TILES, TILES), TILES), :]


def lane_sums(value):
    return lax.dot_general(
        jnp.ones((8, LANES), f32),
        value,
        (((1,), (1,)), ((), ())),
        precision=HIGHEST,
        preferred_element_type=f32,
    )[0:1]


def load_kernel(
    feats_in, gate_in, grad_in, rates_in, residue_in, seg_in,
    feats, grad_scan, squares, table, rates_out, cuts,
    gate, grad, rates, residue, seg, sems, small_sems,
):
    length, width = feats.shape
    small = [
        pltpu.make_async_copy(src, dst, small_sems.at[n])
        for n, (src, dst) in enumerate(((rates_in, rates), (residue_in, residue), (seg_in, seg)))
    ]
    for copy in small:
        copy.start()
    feat_copies = row_copies(feats_in, feats, sems.at[0])
    copies = row_copies(gate_in, gate, sems.at[1]) + row_copies(grad_in, grad, sems.at[2])
    for copy in small:
        copy.wait()
    expand(rates, residue, seg, table, cuts)
    rates_out[...] = rates[...]
    wait_all(feat_copies)
    partial = jnp.zeros((length, LANES), f32)
    for tile in range(width // LANES):
        value = tile_of(feats, 0, tile)
        partial = partial + value * value
    squares[...] = lane_sums(partial)
    wait_all(copies)
    for half in range(HALVES):
        for tile in range(TILES):
            value = tile_of(gate, half, tile) * tile_of(grad, half, tile)
            grad_scan[scan_rows(half, tile, length), :] = value


def mode_params(rates, residue):
    rate = rates[...]
    twice = 2.0 * rate
    series = 1.0 - twice / 6.0
    for n in (5, 4, 3, 2):
        series = 1.0 - twice / n * series
    root = jnp.sqrt(jnp.where(twice < 0.25, twice * series, 1.0 - jnp.exp(-twice)))
    return jnp.concatenate([rate, residue[...] * root, root], axis=0)


def spread_groups(packed, width, first):
    group_count = packed.shape[1]
    group = lax.broadcasted_iota(jnp.int32, (group_count, width), 0)
    lane = lax.broadcasted_iota(jnp.int32, (group_count, width), 1)
    spread = jnp.where(first(lane) == group, 1.0, 0.0).astype(jnp.bfloat16)
    return exact_dot(packed, spread)


def own_mode(value):
    row = lax.broadcasted_iota(jnp.int32, value.shape, 0)
    lane = lax.broadcasted_iota(jnp.int32, value.shape, 1)
    return jnp.sum(jnp.where(row == lane % GROUP, value, 0.0), axis=0, keepdims=True)


def expand(rates, residue, seg, table, cuts):
    width = table.shape[1] * LANES
    full = spread_groups(mode_params(rates, residue), width, lambda lane: lane // GROUP)
    for tile in range(width // LANES):
        at = slice(tile * LANES, (tile + 1) * LANES)
        table[:, tile, :] = full[0 : 2 * MODES, at]
    for p in range(COUNT - 1):
        cuts[p] = jnp.sum(jnp.where(seg[...] <= p, 1, 0))
    cuts[COUNT - 1] = seg.shape[1]


def adjoint_kernel(cuts, grad_scan, rates, adj):
    length = grad_scan.shape[0] // (HALVES * TILES)
    edge = jnp.int32(length)
    for p in range(COUNT - 1):
        edge = jnp.minimum(edge, jnp.where(cuts[p] > 0, cuts[p], length))
    first = lax.broadcasted_iota(jnp.int32, (length, LANES), 0) < edge
    lag = lax.broadcasted_iota(jnp.int32, (MODES, LANES), 1).astype(f32)
    rate = rates[...]
    further = jnp.exp(-float(LANES) * rate)
    share = LANES // GROUP
    row = lax.broadcasted_iota(jnp.int32, (LANES, LANES), 0) // MODES
    own = row == lax.broadcasted_iota(jnp.int32, (LANES, LANES), 1) // GROUP
    dot = lambda x, y: jnp.dot(x, y, preferred_element_type=f32)
    for tile in range(HALVES * TILES):
        value = grad_scan[scan_rows(tile // TILES, tile % TILES, length), :]
        high, low = split(jnp.where(first, value, 0.0))
        blocks = []
        for group in range(tile * share, (tile + 1) * share):
            parts = [jnp.exp(-lag * rate[:, group : group + 1])]
            for _ in range(length // LANES - 1):
                parts.append(parts[-1] * further[:, group : group + 1])
            blocks.append(jnp.concatenate(parts, axis=1))
        near, far = split(jnp.concatenate(blocks, axis=0))
        full = dot(near, high) + (dot(far, high) + dot(near, low))
        full = jnp.where(own, full, 0.0)
        adj[tile * MODES : (tile + 1) * MODES, :] = tree(
            [full[n * MODES : (n + 1) * MODES, :] for n in range(share)]
        )


def state_kernel(
    full_width, seg, cuts, feats, grad_scan, part0, part1, part2, part3, table, gain, adj,
    msg_out, inverse, grad_out, msg, feat_scan, ends, sums, sems, grad_sems,
):
    length = feats.shape[0]
    grad_copies = row_copies(grad_scan, grad_out, grad_sems)
    inverse[...] = inverse_of((part0, part1, part2, part3), full_width)
    scale = column(inverse[...])
    share = msg.shape[0] // HALVES

    def send(half):
        at = pl.ds(half * share, share)
        return pltpu.make_async_copy(msg.at[at, :], msg_out.at[at, :], sems.at[half])

    for half in range(HALVES):
        state_half(
            length, half, scale, seg, cuts, feats, grad_scan, table, gain, adj,
            msg, feat_scan, ends, sums,
        )
        send(half).start()
    for half in range(HALVES):
        send(half).wait()
    wait_all(grad_copies)


def state_half(
    length, half, scale, seg, cuts, feats, grad_scan, table, gain, adj,
    msg, feat_scan, ends, sums,
):
    for tile in range(TILES):
        feat_scan[scan_rows(0, tile, length), :] = tile_of(feats, half, tile) * scale
    decay = decay_of(table, half)

    def step(t, carry, keep):
        value = row_at(feat_scan, 0, length, t)
        grads = row_at(grad_scan, half, length, t)
        states = [decayed(decay[r], carry[r], keep) + value for r in range(MODES)]
        totals = [carry[MODES + r] + grads * states[r] for r in range(MODES)]
        return tuple(states) + tuple(totals)

    zero = jnp.zeros((TILES, LANES), f32)
    carry = scan(length, seg, cuts, step, (zero,) * (2 * MODES), False)
    gains = gain[pl.ds(pl.multiple_of(half * TILES, TILES), TILES), :]
    weights = weight_of(table, half)
    for r in range(MODES):
        ends[pl.ds(r, TILES, stride=MODES), :] = carry[r]
        sums[r * TILES : (r + 1) * TILES, :] = carry[MODES + r] * gains
    gain_row = tree([weights[r] * carry[MODES + r] for r in range(MODES)])
    spread = exact_dot(sums[...], block_ones())
    lane_mode = lane_iota(TILES) % GROUP
    mode_row = tree(
        [
            jnp.where(lane_mode == r, spread[r * TILES : (r + 1) * TILES, :], 0.0)
            for r in range(MODES)
        ]
    )
    even = join(gain_row, swap(mode_row))
    odd = join(swap(gain_row), mode_row)
    first = jnp.full((1, LANES), seg[0, 0], jnp.int32).astype(f32)
    last = jnp.full((1, LANES), seg[0, length - 1], jnp.int32).astype(f32)
    near = join(first, last)

    for tile in range(TILES):
        state = ends[tile * MODES : (tile + 1) * MODES, :]
        own = (half * TILES + tile) * MODES
        adjoint = adj[pl.ds(pl.multiple_of(own, MODES), MODES), :]
        at = 2 * (half * TILES + tile) * ROWS
        msg[at : at + MODES, :] = join(state, swap(adjoint))
        msg[at + MODES : at + MODES + 1, :] = even[tile : tile + 1, :]
        msg[at + MODES + 1 : at + ROWS, :] = near
        at += ROWS
        msg[at : at + MODES, :] = join(swap(state), adjoint)
        msg[at + MODES : at + MODES + 1, :] = odd[tile : tile + 1, :]
        msg[at + MODES + 1 : at + ROWS, :] = near


def carry_kernel(
    span, norm_factor, own, msg, rates, residue, gain, out_hbm, out, carries, sems
):
    count = msg.shape[0] // ROWS
    share = rates.shape[1] // count
    first = own[0] * share
    full = spread_groups(
        mode_params(rates, residue), LANES, lambda lane: first + lane % (LANES // 2) // GROUP
    )
    rate, weight = full[0:MODES], full[MODES : 2 * MODES]
    root = own_mode(full[2 * MODES :])
    at = pl.ds(pl.multiple_of(own[0] // 2 * LANES, LANES), LANES)
    gains = gain[:, at]
    odd = own[0] % 2 == 1
    gains = jnp.where(odd, join(swap(gains), gains), join(gains, swap(gains)))
    single = jnp.exp(-rate)
    whole = jnp.exp(-rate * float(span))
    state = jnp.zeros((MODES, LANES), f32)
    before = None
    ends = [msg[i * ROWS : i * ROWS + MODES, :] for i in range(count)]
    ids = [msg[i * ROWS + MODES + 1 : (i + 1) * ROWS, :] for i in range(count)]
    for m in range(count):
        other = count - 1 - m
        fresh = join(ends[m], ends[other])
        near = join(ids[m], ids[other])
        far = join(swap(ids[m]), swap(ids[other]))
        if before is None:
            carries[m] = state
            state = fresh
        else:
            carries[m] = jnp.where(near == before, state, 0.0)
            state = fresh + jnp.where(far == before, whole * state, 0.0)
        before = far
    total = jnp.zeros((MODES, LANES), f32)
    row = jnp.zeros((1, LANES), f32)
    for i in range(count):
        carried = join(carries[i], carries[count - 1 - i])
        out[i * ROWS : i * ROWS + MODES, :] = carried
        total = total + carried * swap(ends[i])
        row = row + msg[i * ROWS + MODES : i * ROWS + MODES + 1, :]
    total = total * single
    gain_row = jnp.sum(weight * total, axis=0, keepdims=True)
    spread = exact_dot(total * gains, block_ones())
    pick = lane_iota(MODES) % GROUP == lax.broadcasted_iota(jnp.int32, (MODES, LANES), 0)
    mode_row = jnp.sum(jnp.where(pick, spread, 0.0), axis=0, keepdims=True)
    row = (row + join(gain_row, swap(mode_row))) * join(jnp.ones((1, LANES), f32), root)
    row = row * norm_factor
    modes = join(own_mode(rate), own_mode(weight))
    for i in range(count):
        out[i * ROWS + MODES : i * ROWS + MODES + 1, :] = row
        out[i * ROWS + MODES + 1 : (i + 1) * ROWS, :] = modes
    copies = []
    part = out.shape[0] // COPIES
    for i in range(COPIES):
        at = pl.ds(i * part, part)
        copies.append(pltpu.make_async_copy(out.at[at, :], out_hbm.at[at, :], sems.at[i]))
        copies[-1].start()
    for copy in copies:
        copy.wait()


def local_kernel(backward, seg, cuts, table_in, *refs):
    if backward:
        grad_in, feats_in, gain, out, inner, feats, result, feat_sems, *rest = refs
        value_out, sems, partial, grad_scan, grad_sems, table, table_sem = rest
        table_copy = pltpu.make_async_copy(table_in, table, table_sem.at[0])
        table_copy.start()
        grad_copies = row_copies(grad_in, grad_scan, grad_sems)
    else:
        feats_in, inverse, value_out, table_out, result, feat_sems, scan_in, feats, table_sem = refs
        table = table_in
        table_copy = pltpu.make_async_copy(table, table_out, table_sem.at[0])
        table_copy.start()
    length = seg.shape[1]
    feat_copies = row_copies(feats_in, feats, feat_sems)
    if not backward:
        scale = column(inverse[...])
        wait_all(feat_copies)
    copies = []
    for half in range(HALVES):
        if backward:
            values, at_half = grad_scan, half
            part = COPIES // HALVES
            wait_all(grad_copies[half * part : (half + 1) * part])
            if half == 0:
                table_copy.wait()
        else:
            values, at_half = scan_in, 0
            for tile in range(TILES):
                values[scan_rows(0, tile, length), :] = tile_of(feats, half, tile) * scale
        decay = decay_of(table, half)
        weight = weight_of(table, half)

        def step(t, states, keep):
            value = row_at(values, at_half, length, t)
            states = tuple(decayed(decay[r], states[r], keep) + value for r in range(MODES))
            result[pl.ds(pl.multiple_of(t * TILES, TILES), TILES), :] = tree(
                [weight[r] * states[r] for r in range(MODES)]
            )
            return states

        zero = jnp.zeros((TILES, LANES), f32)
        scan(length, seg, cuts, step, (zero,) * MODES, backward)
        for tile in range(TILES):
            value_out[:, lanes_of(half, tile)] = result[pl.ds(tile, length, stride=TILES), :]
        if backward:
            at = pl.ds(half * TILES * LANES, TILES * LANES)
            copies.append(pltpu.make_async_copy(value_out.at[:, at], out.at[:, at], sems.at[half]))
            copies[-1].start()
    if backward:
        wait_all(feat_copies)
        inner[...] = inner_sums(value_out, feats, gain, partial)
    else:
        table_copy.wait()
    wait_all(copies)


def inner_sums(value, feats, gain, partial):
    length, width = feats.shape
    step = length // BLOCKS
    for i in range(BLOCKS):
        here = slice(i * step, (i + 1) * step)
        partial[here, :] = tree(
            [
                value[here, at] * gain[:, at] * feats[here, at].astype(f32)
                for at in tiles_at(width)
            ]
        )
    return lane_sums(partial[...])


def from_owners(back, pair, rows, upper):
    parts = []
    for n in range(2):
        first = (4 * pair + 2 * n) * ROWS
        low = back[first + rows.start : first + rows.stop, :]
        high = back[first + ROWS + rows.start : first + ROWS + rows.stop, :]
        parts.append(join(swap(low), high) if upper else join(low, swap(high)))
    return jnp.concatenate(parts, axis=1)


def powers(cuts, back, pair, length, ahead):
    t = lax.broadcasted_iota(jnp.int32, (length, WIDE), 0)
    modes = slice(MODES + 1, MODES + 2)
    rate = from_owners(back, pair, modes, False)
    weight = from_owners(back, pair, modes, True)
    sub = lax.broadcasted_iota(jnp.int32, (8, WIDE), 0).astype(f32)
    further = jnp.exp(-8.0 * rate)
    if ahead:
        edge = jnp.int32(0)
        for p in range(COUNT - 1):
            edge = jnp.maximum(edge, jnp.where(cuts[p] < length, cuts[p], 0))
        linked = t >= edge
        lag = 8.0 - sub
    else:
        edge = jnp.int32(length)
        for p in range(COUNT - 1):
            edge = jnp.minimum(edge, jnp.where(cuts[p] > 0, cuts[p], length))
        linked = t < edge
        lag = sub + 1.0
    blocks = [jnp.exp(-lag * rate) * weight]
    for _ in range(length // 8 - 1):
        blocks.append(blocks[-1] * further)
    power = jnp.concatenate(blocks[::-1] if ahead else blocks, axis=0)
    return split(jnp.where(linked, power, 0.0))


def split(value):
    high = value.astype(jnp.bfloat16)
    return high, (value - high.astype(f32)).astype(jnp.bfloat16)


def from_carry(cuts, back, pair, length, ahead):
    carry = from_owners(back, pair, slice(0, MODES), ahead)
    own = lax.broadcasted_iota(jnp.int32, (WIDE, WIDE), 0) // MODES == (
        lax.broadcasted_iota(jnp.int32, (WIDE, WIDE), 1) // GROUP
    )

    def spread(value):
        value = jnp.concatenate([value.astype(f32)] * (WIDE // MODES), axis=0)
        return jnp.where(own, value, 0.0).astype(jnp.bfloat16)

    high, low = (spread(value) for value in split(carry))
    near, far = powers(cuts, back, pair, length, ahead)
    dot = lambda x, y: jnp.dot(x, y, preferred_element_type=f32)
    return dot(near, high) + (dot(far, high) + dot(near, low))


def row_copy(src, dst, sems, part, parts=COPIES):
    step = dst.shape[0] // parts
    at = pl.ds(part * step, step)
    return pltpu.make_async_copy(src.at[at, :], dst.at[at, :], sems.at[part])


def row_copies(src, dst, sems, parts=COPIES):
    copies = [row_copy(src, dst, sems, part, parts) for part in range(parts)]
    for copy in copies:
        copy.start()
    return copies


def wait_all(copies):
    for copy in copies:
        copy.wait()


def tiles_at(width):
    return [slice(tile * LANES, (tile + 1) * LANES) for tile in range(width // LANES)]


def backward_kernel(
    cuts, back, inner_local, feats, gain, gate_in, grad_in,
    carried, inner, totals, gate, grad, partial, sems,
):
    length, width = feats.shape
    copies = []
    for n, (src, dst) in enumerate(((gate_in, gate), (grad_in, grad))):
        copies += row_copies(src, dst, sems.at[n], 1)
    for n in range(totals.shape[0]):
        totals[n : n + 1, :] = back[n * ROWS + MODES : n * ROWS + MODES + 1, :]
    for pair in range(width // WIDE):
        at = slice(pair * WIDE, (pair + 1) * WIDE)
        carried[:, at] = from_carry(cuts, back, pair, length, True)
    inner[...] = inner_local[...] + inner_sums(carried, feats, gain, partial)
    wait_all(copies)


def forward_kernel(
    cuts, back, local, gate, grad, gain, mixed, grad_gate, carried
):
    length, width = gate.shape
    for pair in range(width // WIDE):
        at = slice(pair * WIDE, (pair + 1) * WIDE)
        carried[:, at] = from_carry(cuts, back, pair, length, False)
    step = length // BLOCKS
    for i in range(BLOCKS):
        here = slice(i * step, (i + 1) * step)
        for at in tiles_at(width):
            conv = (local[here, at] + carried[here, at]) * gain[:, at]
            mixed[here, at] = (gate[here, at].astype(f32) * conv).astype(jnp.bfloat16)
            grad_gate[here, at] = (grad[here, at].astype(f32) * conv).astype(jnp.bfloat16)


def feature_kernel(
    full_width, local, carried, feats, gain, inverse, i0, i1, i2, i3, own, other, mixed_v, grad_gate_v,
    out, modes, gains, mixed, grad_gate, out_v, sems, gate_sems,
):
    length, width = feats.shape
    gate_copies = row_copies(mixed_v, mixed, gate_sems.at[0])
    gate_copies += row_copies(grad_gate_v, grad_gate, gate_sems.at[1])
    scale = column(inverse[...])
    factor = column(total_row((i0, i1, i2, i3))) * scale * scale / full_width
    copies = []
    step = length // BLOCKS
    for i in range(BLOCKS):
        here = slice(i * step, (i + 1) * step)
        for at in tiles_at(width):
            scaled = (local[here, at] + carried[here, at]) * gain[:, at]
            value = scale[here] * (scaled - feats[here, at].astype(f32) * factor[here])
            out_v[here, at] = value.astype(jnp.bfloat16)
        if (i + 1) % (BLOCKS // COPIES) == 0:
            copies.append(row_copy(out_v, out, sems, (i + 1) // (BLOCKS // COPIES) - 1))
            copies[-1].start()

    total = own[...] + other[...]
    count = total.shape[0]
    groups = modes.shape[1]
    share = groups // count
    slot = lax.broadcasted_iota(jnp.int32, (count, groups), 1) // share
    pick = jnp.where(slot == lax.broadcasted_iota(jnp.int32, (count, groups), 0), 1.0, 0.0)
    spread = lax.dot_general(
        total,
        pick.astype(f32),
        (((0,), (0,)), ((), ())),
        precision=HIGHEST,
        preferred_element_type=f32,
    )
    member = lax.broadcasted_iota(jnp.int32, (MODES, groups), 1) % share
    parts = [
        jnp.where(member == n, spread[LANES // 2 + n * MODES : LANES // 2 + (n + 1) * MODES], 0.0)
        for n in range(share)
    ]
    modes[...] = tree(parts)
    for n in range(count // 2):
        gains[n : n + 1, :] = join(total[2 * n : 2 * n + 1, :], swap(total[2 * n + 1 : 2 * n + 2, :]))
    wait_all(copies + gate_copies)


def all_parts(value):
    size = lax.axis_size("tensor")
    others = [
        lax.ppermute(value, "tensor", [(i, (i + d) % size) for i in range(size)])
        for d in range(1, size)
    ]
    return [value] + others


def shards(features, gate_in, segments, gain, residue, rates, grad_out):
    _, length, width = features.shape
    group_count, mode_count = rates.shape
    count = lax.axis_size("ctx")
    full_width = width * lax.axis_size("tensor")
    size = lax.axis_size("dp")
    norm_factor = 1.0 / math.sqrt(size * length * count)
    tiles = width // LANES
    gain_table = gain.reshape(tiles, LANES)
    gain_row = gain.reshape(1, width)

    smem = pl.BlockSpec(memory_space=pltpu.SMEM)
    vmem = pl.BlockSpec(memory_space=pltpu.VMEM)
    hbm = pl.BlockSpec(memory_space=pl.ANY)
    here = pltpu.VMEM
    work = length * width * MODES
    wide = (length, width)
    scan_shape = here((length * tiles, LANES), f32)
    message = pltpu.HBM((count * ROWS, LANES), f32)

    def exchange(value):
        value = value.reshape(count, 1, ROWS * LANES)
        return lax.all_to_all(value, "ctx", 0, 0, tiled=True).reshape(message.shape)

    state_scratch = pltpu.VMEM((TILES * MODES, LANES), f32)

    def call(kernel, name, in_specs, out_specs, out_shape, scratch, flops):
        return pl.pallas_call(
            kernel,
            in_specs=in_specs,
            out_specs=out_specs,
            out_shape=out_shape,
            scratch_shapes=scratch,
            compiler_params=pltpu.CompilerParams(vmem_limit_bytes=16 * 1024 * 1024),
            cost_estimate=pl.CostEstimate(
                flops=flops // 10**6, bytes_accessed=1, transcendentals=0
            ),
            name=name,
        )

    def in_hbm(*values):
        return [pltpu.with_memory_space_constraint(value, pltpu.HBM) for value in values]

    raw = in_hbm(features[0], gate_in[0], grad_out[0], rates.T, residue.T, segments)
    dma = pltpu.SemaphoreType.DMA
    feats, grad_scan, squares, table, rates_here, cuts = call(
        load_kernel,
        "load",
        [hbm] * 6,
        [vmem] * 5 + [smem],
        [
            here(wide, jnp.bfloat16),
            scan_shape,
            here((1, length), f32),
            here((2 * mode_count, tiles, LANES), f32),
            here((mode_count, group_count), f32),
            jax.ShapeDtypeStruct((COUNT,), jnp.int32),
        ],
        [
            pltpu.VMEM(wide, jnp.bfloat16),
            pltpu.VMEM(wide, jnp.bfloat16),
            pltpu.VMEM((mode_count, group_count), f32),
            pltpu.VMEM((mode_count, group_count), f32),
            pltpu.VMEM((1, length), jnp.int32),
            dma((3, COPIES)),
            dma((3,)),
        ],
        2 * length * width,
    )(*raw)
    squares = all_parts(squares)

    adjoint = call(
        adjoint_kernel,
        "adjoint",
        [smem] + [vmem] * 2,
        vmem,
        here((tiles * MODES, LANES), f32),
        [],
        2 * work,
    )(cuts, grad_scan, rates_here)

    scan_scratch = pltpu.VMEM((length * TILES, LANES), f32)
    message_scratch = pltpu.VMEM(message.shape, f32)
    msg, inverse, late_grad = call(
        lambda *refs: state_kernel(full_width, *refs),
        "states",
        [smem, smem] + [vmem] * 9,
        [hbm, vmem, hbm],
        [message, here((1, length), f32), pltpu.HBM((length * tiles, LANES), f32)],
        [
            message_scratch,
            scan_scratch,
            state_scratch,
            state_scratch,
            dma((HALVES,)),
            dma((COPIES,)),
        ],
        4 * work,
    )(segments, cuts, feats, grad_scan, *squares, table, gain_table, adjoint)

    def local(backward, cuts, *sources):
        return call(
            lambda *refs: local_kernel(backward, *refs),
            "local_backward" if backward else "local_forward",
            [smem, smem] + ([hbm, hbm, hbm, vmem] if backward else [vmem, hbm, vmem]),
            [hbm, vmem, vmem] if backward else [vmem, hbm],
            [pltpu.HBM(wide, f32), here((1, length), f32), here(wide, jnp.bfloat16)]
            if backward
            else [here(wide, f32), pltpu.HBM(table.shape, f32)],
            [scan_scratch, dma((COPIES,))]
            + (
                [
                    pltpu.VMEM(wide, f32),
                    dma((HALVES,)),
                    pltpu.VMEM((length, LANES), f32),
                    pltpu.VMEM((length * tiles, LANES), f32),
                    dma((COPIES,)),
                    pltpu.VMEM(table.shape, f32),
                    dma((1,)),
                ]
                if backward
                else [scan_scratch, pltpu.VMEM(wide, jnp.bfloat16), dma((1,))]
            ),
            4 * work,
        )(segments, cuts, *sources)

    conv_local, late_table = local(False, cuts, table, raw[0], inverse)
    msg = exchange(msg)
    late_cuts, msg, conv_local = lax.optimization_barrier((cuts, msg, conv_local))

    own = lax.axis_index("ctx").astype(jnp.int32).reshape(1)
    back = call(
        lambda *refs: carry_kernel(length, norm_factor, *refs),
        "carries",
        [smem] + [vmem] * 4,
        hbm,
        message,
        [message_scratch, pltpu.VMEM((count, MODES, LANES), f32), dma((COPIES,))],
        32 * count * MODES * LANES,
    )(own, msg, rates.T, residue.T, gain_row)

    grad_local, inner_local, feats = local(
        True, late_cuts, *in_hbm(late_table, late_grad), raw[0], gain_row
    )
    back = exchange(back)

    matmuls = 3 * 2 * length * width * WIDE
    carried, inner, totals, gate, grad = call(
        backward_kernel,
        "backward",
        [smem] + [vmem] * 4 + [hbm] * 2,
        [vmem] * 5,
        [
            here(wide, f32),
            here((1, length), f32),
            here((count, LANES), f32),
            here(wide, jnp.bfloat16),
            here(wide, jnp.bfloat16),
        ],
        [pltpu.VMEM((length, LANES), f32), dma((2, COPIES))],
        matmuls,
    )(cuts, back, inner_local, feats, gain_row, raw[1], raw[2])
    inner = all_parts(inner)
    other = lax.ppermute(totals, "dp", [(i, (i + 1) % size) for i in range(size)])

    mixed, grad_gate = call(
        forward_kernel,
        "forward",
        [smem] + [vmem] * 5,
        [vmem] * 2,
        [here(wide, jnp.bfloat16)] * 2,
        [pltpu.VMEM(wide, f32)],
        matmuls,
    )(cuts, back, conv_local, gate, grad, gain_row)

    grad_features, grad_residue, grad_gain, mixed, grad_gate = call(
        lambda *refs: feature_kernel(full_width, *refs),
        "features",
        [vmem] * 13,
        [hbm, vmem, vmem, hbm, hbm],
        [
            jax.ShapeDtypeStruct(wide, jnp.bfloat16),
            jax.ShapeDtypeStruct((mode_count, group_count), f32),
            jax.ShapeDtypeStruct((tiles, LANES), f32),
            jax.ShapeDtypeStruct(wide, jnp.bfloat16),
            jax.ShapeDtypeStruct(wide, jnp.bfloat16),
        ],
        [pltpu.VMEM(wide, jnp.bfloat16), dma((COPIES,)), dma((2, COPIES))],
        4 * length * width,
    )(grad_local, carried, feats, gain_row, inverse, *inner, totals, other, mixed, grad_gate)
    return (
        mixed[None],
        grad_features[None],
        grad_gate[None],
        grad_residue.T,
        grad_gain.reshape(width),
    )


def solution(mesh):
    placed = (
        P("dp", "ctx", "tensor"),
        P("dp", "ctx", "tensor"),
        P("dp", "ctx"),
        P("tensor"),
        P("tensor", None),
        P("tensor", None),
        P("dp", "ctx", "tensor"),
    )
    return jax.shard_map(
        shards,
        mesh=mesh,
        in_specs=placed,
        out_specs=(
            P("dp", "ctx", "tensor"),
            P("dp", "ctx", "tensor"),
            P("dp", "ctx", "tensor"),
            P("tensor", None),
            P("tensor"),
        ),
        check_vma=False,
    )
```

```python
import math

import jax
import jax.numpy as jnp
from jax import lax
from jax.experimental import pallas as pl
from jax.experimental.pallas import tpu as pltpu
from jax.sharding import PartitionSpec as P

epsilon = 1e-06
LANES = 128
TILES = 8
HALVES = 2
MODES = 16
GROUP = 16
UNROLL = 32
COUNT = 4
COPIES = 2
BLOCKS = 8
WIDE = 2 * LANES
ROWS = MODES + 2
HIGHEST = lax.Precision.HIGHEST
f32 = jnp.float32


def lane_iota(rows):
    return lax.broadcasted_iota(jnp.int32, (rows, LANES), 1)


def swap(value):
    return pltpu.roll(value, LANES // 2, axis=1)


def join(low, high):
    return jnp.where(lane_iota(low.shape[0]) < LANES // 2, low, high)


def total_row(parts):
    return tree([part[...] for part in parts])


def inverse_of(parts, full_width):
    return lax.rsqrt(total_row(parts) / full_width + epsilon)


def column(row):
    length = row.shape[1]
    row = jnp.broadcast_to(row, (8, length))
    return jnp.broadcast_to(jnp.transpose(row)[:, 0:1], (length, LANES))


def block_ones():
    left = lax.broadcasted_iota(jnp.int32, (LANES, LANES), 0) // GROUP
    right = lax.broadcasted_iota(jnp.int32, (LANES, LANES), 1) // GROUP
    return jnp.where(left == right, 1.0, 0.0).astype(jnp.bfloat16)


def exact_dot(value, ones):
    high = value.astype(jnp.bfloat16).astype(f32)
    middle = (value - high).astype(jnp.bfloat16).astype(f32)
    parts = jnp.concatenate([high, middle, value - high - middle], axis=0)
    full = jnp.dot(parts.astype(jnp.bfloat16), ones, preferred_element_type=f32)
    rows = value.shape[0]
    return full[0:rows] + (full[rows : 2 * rows] + full[2 * rows :])


def lanes_of(half, tile):
    return pl.ds(pl.multiple_of((half * TILES + tile) * LANES, LANES), LANES)


def tile_of(ref, half, tile):
    return ref[:, lanes_of(half, tile)].astype(f32)


def scan_rows(half, tile, length):
    return pl.ds(half * length * TILES + tile, length, stride=TILES)


def table_of(table, half, first):
    at = pl.ds(pl.multiple_of(half * TILES, TILES), TILES)
    return [table[first + r, at, :] for r in range(MODES)]


def decay_of(table, half):
    return [jnp.exp(-rate) for rate in table_of(table, half, 0)]


def weight_of(table, half):
    return table_of(table, half, MODES)


def state_rows(half, r):
    return pl.ds(half * TILES * MODES + r, TILES, stride=MODES)


def tree(values):
    values = list(values)
    while len(values) > 1:
        values = [a + b for a, b in zip(values[::2], values[1::2])]
    return values[0]


def scan(length, seg, cuts, step, carry, backward):
    groups = length // UNROLL

    def run(group, carry, masked):
        base = group * UNROLL
        for u in range(UNROLL):
            t = base + (UNROLL - 1 - u if backward else u)
            keep = None
            if masked:
                near = jnp.minimum(t + 1, length - 1) if backward else jnp.maximum(t - 1, 0)
                keep = seg[0, t] == seg[0, near]
            carry = step(t, carry, keep)
        return carry

    def stretch(p, carry):
        now, states = carry
        if backward:
            cut = jnp.where(p < COUNT - 1, cuts[jnp.maximum(COUNT - 2 - p, 0)], 0)
            group = (cut - 1) // UNROLL
            stop = jnp.where(
                cut >= length, now, jnp.where(cut <= 0, 0, jnp.minimum(now, group + 1))
            )
            states = lax.fori_loop(
                0, now - stop, lambda i, value: run(now - 1 - i, value, False), states
            )
            broken = (cut > 0) & (cut < length) & (group < now)
            after = group
        else:
            cut = jnp.where(p < COUNT - 1, cuts[jnp.minimum(p, COUNT - 2)], length)
            group = cut // UNROLL
            stop = jnp.where(
                cut <= 0, now, jnp.where(cut >= length, groups, jnp.maximum(now, group))
            )
            states = lax.fori_loop(now, stop, lambda i, value: run(i, value, False), states)
            broken = (cut > 0) & (cut < length) & (group >= now)
            after = group + 1
        states = lax.cond(
            broken, lambda value: run(group, value, True), lambda value: value, states
        )
        return jnp.where(broken, after, stop), states

    def general(carry):
        start = jnp.int32(groups if backward else 0)
        return lax.fori_loop(0, COUNT, stretch, (start, carry))[1]

    def unbroken(carry):
        def body(i, carry):
            return run(groups - 1 - i if backward else i, carry, False)

        return lax.fori_loop(0, groups, body, carry)

    broken = cuts[0] < 0
    for p in range(COUNT - 1):
        broken = broken | ((cuts[p] > 0) & (cuts[p] < length))
    return lax.cond(broken, general, unbroken, carry)


def decayed(decay, state, keep):
    state = decay * state
    return state if keep is None else jnp.where(keep, state, 0.0)


def row_at(ref, half, length, t):
    return ref[pl.ds(pl.multiple_of((half * length + t) * TILES, TILES), TILES), :]


def lane_sums(value):
    high = value.astype(jnp.bfloat16)
    rest = value - high.astype(f32)
    middle = rest.astype(jnp.bfloat16)
    low = (rest - middle.astype(f32)).astype(jnp.bfloat16)
    ones = jnp.ones((16, LANES), jnp.bfloat16)
    sums = [
        lax.dot_general(ones, part, (((1,), (1,)), ((), ())), preferred_element_type=f32)
        for part in (high, middle, low)
    ]
    return (sums[0] + (sums[1] + sums[2]))[0:1]


def load_kernel(
    feats_in, gate_in, grad_in, rates_in, residue_in, seg_in,
    feats, grad_scan, squares, table, rates_out, cuts,
    gate, grad, rates, residue, seg, sems, small_sems,
):
    length, width = feats.shape
    small = [
        pltpu.make_async_copy(src, dst, small_sems.at[n])
        for n, (src, dst) in enumerate(((rates_in, rates), (residue_in, residue), (seg_in, seg)))
    ]
    for copy in small:
        copy.start()
    feat_copies = row_copies(feats_in, feats, sems.at[0], 1)
    copies = row_copies(gate_in, gate, sems.at[1], 1) + row_copies(grad_in, grad, sems.at[2], 1)
    for copy in small:
        copy.wait()
    expand(rates, residue, seg, table, cuts)
    rates_out[...] = rates[...]
    wait_all(feat_copies)
    partial = jnp.zeros((length, LANES), f32)
    for tile in range(width // LANES):
        value = tile_of(feats, 0, tile)
        partial = partial + value * value
    squares[...] = lane_sums(partial)
    wait_all(copies)
    for half in range(HALVES):
        for tile in range(TILES):
            value = tile_of(gate, half, tile) * tile_of(grad, half, tile)
            grad_scan[scan_rows(half, tile, length), :] = value


def mode_params(rates, residue):
    rate = rates[...]
    twice = 2.0 * rate
    series = 1.0 - twice / 6.0
    for n in (5, 4, 3, 2):
        series = 1.0 - twice / n * series
    root = jnp.sqrt(jnp.where(twice < 0.25, twice * series, 1.0 - jnp.exp(-twice)))
    return jnp.concatenate([rate, residue[...] * root, root], axis=0)


def spread_groups(packed, width, first):
    group_count = packed.shape[1]
    group = lax.broadcasted_iota(jnp.int32, (group_count, width), 0)
    lane = lax.broadcasted_iota(jnp.int32, (group_count, width), 1)
    spread = jnp.where(first(lane) == group, 1.0, 0.0).astype(jnp.bfloat16)
    return exact_dot(packed, spread)


def own_mode(value):
    row = lax.broadcasted_iota(jnp.int32, value.shape, 0)
    lane = lax.broadcasted_iota(jnp.int32, value.shape, 1)
    return jnp.sum(jnp.where(row == lane % GROUP, value, 0.0), axis=0, keepdims=True)


def expand(rates, residue, seg, table, cuts):
    width = table.shape[1] * LANES
    full = spread_groups(mode_params(rates, residue), width, lambda lane: lane // GROUP)
    for tile in range(width // LANES):
        at = slice(tile * LANES, (tile + 1) * LANES)
        table[:, tile, :] = full[0 : 2 * MODES, at]
    for p in range(COUNT - 1):
        cuts[p] = jnp.sum(jnp.where(seg[...] <= p, 1, 0))
    cuts[COUNT - 1] = seg.shape[1]


def adjoint_kernel(cuts, grad_scan, rates, adj):
    length = grad_scan.shape[0] // (HALVES * TILES)
    edge = jnp.int32(length)
    for p in range(COUNT - 1):
        edge = jnp.minimum(edge, jnp.where(cuts[p] > 0, cuts[p], length))
    first = lax.broadcasted_iota(jnp.int32, (length, LANES), 0) < edge
    lag = lax.broadcasted_iota(jnp.int32, (MODES, LANES), 1).astype(f32)
    rate = rates[...]
    further = jnp.exp(-float(LANES) * rate)
    share = LANES // GROUP
    row = lax.broadcasted_iota(jnp.int32, (LANES, LANES), 0) // MODES
    own = row == lax.broadcasted_iota(jnp.int32, (LANES, LANES), 1) // GROUP
    dot = lambda x, y: jnp.dot(x, y, preferred_element_type=f32)
    for tile in range(HALVES * TILES):
        value = grad_scan[scan_rows(tile // TILES, tile % TILES, length), :]
        high, low = split(jnp.where(first, value, 0.0))
        blocks = []
        for group in range(tile * share, (tile + 1) * share):
            parts = [jnp.exp(-lag * rate[:, group : group + 1])]
            for _ in range(length // LANES - 1):
                parts.append(parts[-1] * further[:, group : group + 1])
            blocks.append(jnp.concatenate(parts, axis=1))
        near, far = split(jnp.concatenate(blocks, axis=0))
        full = dot(near, high) + (dot(far, high) + dot(near, low))
        full = jnp.where(own, full, 0.0)
        adj[tile * MODES : (tile + 1) * MODES, :] = tree(
            [full[n * MODES : (n + 1) * MODES, :] for n in range(share)]
        )


def state_kernel(
    full_width, seg, cuts, feats, grad_scan, part0, part1, part2, part3, table, gain, adj,
    msg_out, inverse, grad_out, msg, feat_scan, ends, sums, sems, grad_sems,
):
    length = feats.shape[0]
    grad_copies = row_copies(grad_scan, grad_out, grad_sems, 1)
    inverse[...] = inverse_of((part0, part1, part2, part3), full_width)
    scale = column(inverse[...])
    share = msg.shape[0] // HALVES

    def send(half):
        at = pl.ds(half * share, share)
        return pltpu.make_async_copy(msg.at[at, :], msg_out.at[at, :], sems.at[half])

    for half in range(HALVES):
        state_half(
            length, half, scale, seg, cuts, feats, grad_scan, table, gain, adj,
            msg, feat_scan, ends, sums,
        )
        send(half).start()
    for half in range(HALVES):
        send(half).wait()
    wait_all(grad_copies)


def state_half(
    length, half, scale, seg, cuts, feats, grad_scan, table, gain, adj,
    msg, feat_scan, ends, sums,
):
    for tile in range(TILES):
        feat_scan[scan_rows(0, tile, length), :] = tile_of(feats, half, tile) * scale
    decay = decay_of(table, half)

    def step(t, carry, keep):
        value = row_at(feat_scan, 0, length, t)
        grads = row_at(grad_scan, half, length, t)
        states = [decayed(decay[r], carry[r], keep) + value for r in range(MODES)]
        totals = [carry[MODES + r] + grads * states[r] for r in range(MODES)]
        return tuple(states) + tuple(totals)

    zero = jnp.zeros((TILES, LANES), f32)
    carry = scan(length, seg, cuts, step, (zero,) * (2 * MODES), False)
    gains = gain[pl.ds(pl.multiple_of(half * TILES, TILES), TILES), :]
    weights = weight_of(table, half)
    for r in range(MODES):
        ends[pl.ds(r, TILES, stride=MODES), :] = carry[r]
        sums[r * TILES : (r + 1) * TILES, :] = carry[MODES + r] * gains
    gain_row = tree([weights[r] * carry[MODES + r] for r in range(MODES)])
    spread = exact_dot(sums[...], block_ones())
    lane_mode = lane_iota(TILES) % GROUP
    mode_row = tree(
        [
            jnp.where(lane_mode == r, spread[r * TILES : (r + 1) * TILES, :], 0.0)
            for r in range(MODES)
        ]
    )
    even = join(gain_row, swap(mode_row))
    odd = join(swap(gain_row), mode_row)
    first = jnp.full((1, LANES), seg[0, 0], jnp.int32).astype(f32)
    last = jnp.full((1, LANES), seg[0, length - 1], jnp.int32).astype(f32)
    near = join(first, last)

    for tile in range(TILES):
        state = ends[tile * MODES : (tile + 1) * MODES, :]
        own = (half * TILES + tile) * MODES
        adjoint = adj[pl.ds(pl.multiple_of(own, MODES), MODES), :]
        at = 2 * (half * TILES + tile) * ROWS
        msg[at : at + MODES, :] = join(state, swap(adjoint))
        msg[at + MODES : at + MODES + 1, :] = even[tile : tile + 1, :]
        msg[at + MODES + 1 : at + ROWS, :] = near
        at += ROWS
        msg[at : at + MODES, :] = join(swap(state), adjoint)
        msg[at + MODES : at + MODES + 1, :] = odd[tile : tile + 1, :]
        msg[at + MODES + 1 : at + ROWS, :] = near


def carry_kernel(
    span, norm_factor, own, msg, rates, residue, gain, out_hbm, out, carries, sems
):
    count = msg.shape[0] // ROWS
    share = rates.shape[1] // count
    first = own[0] * share
    full = spread_groups(
        mode_params(rates, residue), LANES, lambda lane: first + lane % (LANES // 2) // GROUP
    )
    rate, weight = full[0:MODES], full[MODES : 2 * MODES]
    root = own_mode(full[2 * MODES :])
    at = pl.ds(pl.multiple_of(own[0] // 2 * LANES, LANES), LANES)
    gains = gain[:, at]
    odd = own[0] % 2 == 1
    gains = jnp.where(odd, join(swap(gains), gains), join(gains, swap(gains)))
    single = jnp.exp(-rate)
    whole = jnp.exp(-rate * float(span))
    state = jnp.zeros((MODES, LANES), f32)
    before = None
    ends = [msg[i * ROWS : i * ROWS + MODES, :] for i in range(count)]
    ids = [msg[i * ROWS + MODES + 1 : (i + 1) * ROWS, :] for i in range(count)]
    for m in range(count):
        other = count - 1 - m
        fresh = join(ends[m], ends[other])
        near = join(ids[m], ids[other])
        far = join(swap(ids[m]), swap(ids[other]))
        if before is None:
            carries[m] = state
            state = fresh
        else:
            carries[m] = jnp.where(near == before, state, 0.0)
            state = fresh + jnp.where(far == before, whole * state, 0.0)
        before = far
    total = jnp.zeros((MODES, LANES), f32)
    row = jnp.zeros((1, LANES), f32)
    for i in range(count):
        carried = join(carries[i], carries[count - 1 - i])
        out[i * ROWS : i * ROWS + MODES, :] = carried
        total = total + carried * swap(ends[i])
        row = row + msg[i * ROWS + MODES : i * ROWS + MODES + 1, :]
    total = total * single
    gain_row = jnp.sum(weight * total, axis=0, keepdims=True)
    spread = exact_dot(total * gains, block_ones())
    pick = lane_iota(MODES) % GROUP == lax.broadcasted_iota(jnp.int32, (MODES, LANES), 0)
    mode_row = jnp.sum(jnp.where(pick, spread, 0.0), axis=0, keepdims=True)
    row = (row + join(gain_row, swap(mode_row))) * join(jnp.ones((1, LANES), f32), root)
    row = row * norm_factor
    modes = join(own_mode(rate), own_mode(weight))
    for i in range(count):
        out[i * ROWS + MODES : i * ROWS + MODES + 1, :] = row
        out[i * ROWS + MODES + 1 : (i + 1) * ROWS, :] = modes
    copies = []
    part = out.shape[0] // COPIES
    for i in range(COPIES):
        at = pl.ds(i * part, part)
        copies.append(pltpu.make_async_copy(out.at[at, :], out_hbm.at[at, :], sems.at[i]))
        copies[-1].start()
    for copy in copies:
        copy.wait()


def local_kernel(backward, seg, cuts, table_in, *refs):
    if backward:
        grad_in, feats_in, gain, out, inner, feats, result, feat_sems, *rest = refs
        value_out, sems, partial, grad_scan, grad_sems, table, table_sem = rest
        table_copy = pltpu.make_async_copy(table_in, table, table_sem.at[0])
        table_copy.start()
        grad_copies = row_copies(grad_in, grad_scan, grad_sems)
    else:
        feats_in, inverse, value_out, table_out, result, feat_sems, scan_in, feats, table_sem = refs
        table = table_in
        table_copy = pltpu.make_async_copy(table, table_out, table_sem.at[0])
        table_copy.start()
    length = seg.shape[1]
    feat_copies = row_copies(feats_in, feats, feat_sems)
    if not backward:
        scale = column(inverse[...])
        wait_all(feat_copies)
    copies = []
    for half in range(HALVES):
        if backward:
            values, at_half = grad_scan, half
            part = COPIES // HALVES
            wait_all(grad_copies[half * part : (half + 1) * part])
            if half == 0:
                table_copy.wait()
        else:
            values, at_half = scan_in, 0
            for tile in range(TILES):
                values[scan_rows(0, tile, length), :] = tile_of(feats, half, tile) * scale
        decay = decay_of(table, half)
        weight = weight_of(table, half)

        def step(t, states, keep):
            value = row_at(values, at_half, length, t)
            states = tuple(decayed(decay[r], states[r], keep) + value for r in range(MODES))
            result[pl.ds(pl.multiple_of(t * TILES, TILES), TILES), :] = tree(
                [weight[r] * states[r] for r in range(MODES)]
            )
            return states

        zero = jnp.zeros((TILES, LANES), f32)
        scan(length, seg, cuts, step, (zero,) * MODES, backward)
        for tile in range(TILES):
            value_out[:, lanes_of(half, tile)] = result[pl.ds(tile, length, stride=TILES), :]
        if backward:
            at = pl.ds(half * TILES * LANES, TILES * LANES)
            copies.append(pltpu.make_async_copy(value_out.at[:, at], out.at[:, at], sems.at[half]))
            copies[-1].start()
    if backward:
        wait_all(feat_copies)
        inner[...] = inner_sums(value_out, feats, gain, partial)
    else:
        table_copy.wait()
    wait_all(copies)


def inner_sums(value, feats, gain, partial):
    length, width = feats.shape
    step = length // BLOCKS
    for i in range(BLOCKS):
        here = slice(i * step, (i + 1) * step)
        partial[here, :] = tree(
            [
                value[here, at] * gain[:, at] * feats[here, at].astype(f32)
                for at in tiles_at(width)
            ]
        )
    return lane_sums(partial[...])


def from_owners(back, pair, rows, upper):
    parts = []
    for n in range(2):
        first = (4 * pair + 2 * n) * ROWS
        low = back[first + rows.start : first + rows.stop, :]
        high = back[first + ROWS + rows.start : first + ROWS + rows.stop, :]
        parts.append(join(swap(low), high) if upper else join(low, swap(high)))
    return jnp.concatenate(parts, axis=1)


def powers(cuts, back, pair, length, ahead):
    t = lax.broadcasted_iota(jnp.int32, (length, WIDE), 0)
    modes = slice(MODES + 1, MODES + 2)
    rate = from_owners(back, pair, modes, False)
    weight = from_owners(back, pair, modes, True)
    sub = lax.broadcasted_iota(jnp.int32, (8, WIDE), 0).astype(f32)
    further = jnp.exp(-8.0 * rate)
    if ahead:
        edge = jnp.int32(0)
        for p in range(COUNT - 1):
            edge = jnp.maximum(edge, jnp.where(cuts[p] < length, cuts[p], 0))
        linked = t >= edge
        lag = 8.0 - sub
    else:
        edge = jnp.int32(length)
        for p in range(COUNT - 1):
            edge = jnp.minimum(edge, jnp.where(cuts[p] > 0, cuts[p], length))
        linked = t < edge
        lag = sub + 1.0
    blocks = [jnp.exp(-lag * rate) * weight]
    for _ in range(length // 8 - 1):
        blocks.append(blocks[-1] * further)
    power = jnp.concatenate(blocks[::-1] if ahead else blocks, axis=0)
    return split(jnp.where(linked, power, 0.0))


def split(value):
    high = value.astype(jnp.bfloat16)
    return high, (value - high.astype(f32)).astype(jnp.bfloat16)


def from_carry(cuts, back, pair, length, ahead):
    carry = from_owners(back, pair, slice(0, MODES), ahead)
    own = lax.broadcasted_iota(jnp.int32, (WIDE, WIDE), 0) // MODES == (
        lax.broadcasted_iota(jnp.int32, (WIDE, WIDE), 1) // GROUP
    )

    def spread(value):
        value = jnp.concatenate([value.astype(f32)] * (WIDE // MODES), axis=0)
        return jnp.where(own, value, 0.0).astype(jnp.bfloat16)

    high, low = (spread(value) for value in split(carry))
    near, far = powers(cuts, back, pair, length, ahead)
    dot = lambda x, y: jnp.dot(x, y, preferred_element_type=f32)
    return dot(near, high) + (dot(far, high) + dot(near, low))


def row_copy(src, dst, sems, part, parts=COPIES):
    step = dst.shape[0] // parts
    at = pl.ds(part * step, step)
    return pltpu.make_async_copy(src.at[at, :], dst.at[at, :], sems.at[part])


def row_copies(src, dst, sems, parts=COPIES):
    copies = [row_copy(src, dst, sems, part, parts) for part in range(parts)]
    for copy in copies:
        copy.start()
    return copies


def wait_all(copies):
    for copy in copies:
        copy.wait()


def tiles_at(width):
    return [slice(tile * LANES, (tile + 1) * LANES) for tile in range(width // LANES)]


def backward_kernel(
    cuts, back, inner_local, feats, gain, gate_in, grad_in,
    carried, inner, totals, gate, grad, partial, sems,
):
    length, width = feats.shape
    copies = []
    for n, (src, dst) in enumerate(((gate_in, gate), (grad_in, grad))):
        copies += row_copies(src, dst, sems.at[n], 1)
    for n in range(totals.shape[0]):
        totals[n : n + 1, :] = back[n * ROWS + MODES : n * ROWS + MODES + 1, :]
    for pair in range(width // WIDE):
        at = slice(pair * WIDE, (pair + 1) * WIDE)
        carried[:, at] = from_carry(cuts, back, pair, length, True)
    inner[...] = inner_local[...] + inner_sums(carried, feats, gain, partial)
    wait_all(copies)


def forward_kernel(
    cuts, back, local, gate, grad, gain, mixed, grad_gate, carried
):
    length, width = gate.shape
    for pair in range(width // WIDE):
        at = slice(pair * WIDE, (pair + 1) * WIDE)
        carried[:, at] = from_carry(cuts, back, pair, length, False)
    step = length // BLOCKS
    for i in range(BLOCKS):
        here = slice(i * step, (i + 1) * step)
        for at in tiles_at(width):
            conv = (local[here, at] + carried[here, at]) * gain[:, at]
            mixed[here, at] = (gate[here, at].astype(f32) * conv).astype(jnp.bfloat16)
            grad_gate[here, at] = (grad[here, at].astype(f32) * conv).astype(jnp.bfloat16)


def feature_kernel(
    full_width, local, carried, feats, gain, inverse, i0, i1, i2, i3, own, other, mixed_v, grad_gate_v,
    out, modes, gains, mixed, grad_gate, out_v, sems, gate_sems,
):
    length, width = feats.shape
    gate_copies = row_copies(mixed_v, mixed, gate_sems.at[0], 1)
    gate_copies += row_copies(grad_gate_v, grad_gate, gate_sems.at[1], 1)
    scale = column(inverse[...])
    factor = column(total_row((i0, i1, i2, i3))) * scale * scale / full_width
    copies = []
    step = length // BLOCKS
    for i in range(BLOCKS):
        here = slice(i * step, (i + 1) * step)
        for at in tiles_at(width):
            scaled = (local[here, at] + carried[here, at]) * gain[:, at]
            value = scale[here] * (scaled - feats[here, at].astype(f32) * factor[here])
            out_v[here, at] = value.astype(jnp.bfloat16)
        if (i + 1) % (BLOCKS // COPIES) == 0:
            copies.append(row_copy(out_v, out, sems, (i + 1) // (BLOCKS // COPIES) - 1))
            copies[-1].start()

    total = own[...] + other[...]
    count = total.shape[0]
    groups = modes.shape[1]
    share = groups // count
    slot = lax.broadcasted_iota(jnp.int32, (count, groups), 1) // share
    pick = jnp.where(slot == lax.broadcasted_iota(jnp.int32, (count, groups), 0), 1.0, 0.0)
    spread = lax.dot_general(
        total,
        pick.astype(f32),
        (((0,), (0,)), ((), ())),
        precision=HIGHEST,
        preferred_element_type=f32,
    )
    member = lax.broadcasted_iota(jnp.int32, (MODES, groups), 1) % share
    parts = [
        jnp.where(member == n, spread[LANES // 2 + n * MODES : LANES // 2 + (n + 1) * MODES], 0.0)
        for n in range(share)
    ]
    modes[...] = tree(parts)
    for n in range(count // 2):
        gains[n : n + 1, :] = join(total[2 * n : 2 * n + 1, :], swap(total[2 * n + 1 : 2 * n + 2, :]))
    wait_all(copies + gate_copies)


def all_parts(value):
    size = lax.axis_size("tensor")
    others = [
        lax.ppermute(value, "tensor", [(i, (i + d) % size) for i in range(size)])
        for d in range(1, size)
    ]
    return [value] + others


def shards(features, gate_in, segments, gain, residue, rates, grad_out):
    _, length, width = features.shape
    group_count, mode_count = rates.shape
    count = lax.axis_size("ctx")
    full_width = width * lax.axis_size("tensor")
    size = lax.axis_size("dp")
    norm_factor = 1.0 / math.sqrt(size * length * count)
    tiles = width // LANES
    gain_table = gain.reshape(tiles, LANES)
    gain_row = gain.reshape(1, width)

    smem = pl.BlockSpec(memory_space=pltpu.SMEM)
    vmem = pl.BlockSpec(memory_space=pltpu.VMEM)
    hbm = pl.BlockSpec(memory_space=pl.ANY)
    here = pltpu.VMEM
    work = length * width * MODES
    wide = (length, width)
    scan_shape = here((length * tiles, LANES), f32)
    message = pltpu.HBM((count * ROWS, LANES), f32)

    def exchange(value):
        value = value.reshape(count, 1, ROWS * LANES)
        return lax.all_to_all(value, "ctx", 0, 0, tiled=True).reshape(message.shape)

    state_scratch = pltpu.VMEM((TILES * MODES, LANES), f32)

    def call(kernel, name, in_specs, out_specs, out_shape, scratch, flops):
        return pl.pallas_call(
            kernel,
            in_specs=in_specs,
            out_specs=out_specs,
            out_shape=out_shape,
            scratch_shapes=scratch,
            compiler_params=pltpu.CompilerParams(vmem_limit_bytes=16 * 1024 * 1024),
            cost_estimate=pl.CostEstimate(
                flops=flops // 10**6, bytes_accessed=1, transcendentals=0
            ),
            name=name,
        )

    def in_hbm(*values):
        return [pltpu.with_memory_space_constraint(value, pltpu.HBM) for value in values]

    raw = in_hbm(features[0], gate_in[0], grad_out[0], rates.T, residue.T, segments)
    dma = pltpu.SemaphoreType.DMA
    feats, grad_scan, squares, table, rates_here, cuts = call(
        load_kernel,
        "load",
        [hbm] * 6,
        [vmem] * 5 + [smem],
        [
            here(wide, jnp.bfloat16),
            scan_shape,
            here((1, length), f32),
            here((2 * mode_count, tiles, LANES), f32),
            here((mode_count, group_count), f32),
            jax.ShapeDtypeStruct((COUNT,), jnp.int32),
        ],
        [
            pltpu.VMEM(wide, jnp.bfloat16),
            pltpu.VMEM(wide, jnp.bfloat16),
            pltpu.VMEM((mode_count, group_count), f32),
            pltpu.VMEM((mode_count, group_count), f32),
            pltpu.VMEM((1, length), jnp.int32),
            dma((3, COPIES)),
            dma((3,)),
        ],
        2 * length * width,
    )(*raw)
    squares = all_parts(squares)

    adjoint = call(
        adjoint_kernel,
        "adjoint",
        [smem] + [vmem] * 2,
        vmem,
        here((tiles * MODES, LANES), f32),
        [],
        2 * work,
    )(cuts, grad_scan, rates_here)

    scan_scratch = pltpu.VMEM((length * TILES, LANES), f32)
    message_scratch = pltpu.VMEM(message.shape, f32)
    msg, inverse, late_grad = call(
        lambda *refs: state_kernel(full_width, *refs),
        "states",
        [smem, smem] + [vmem] * 9,
        [hbm, vmem, hbm],
        [message, here((1, length), f32), pltpu.HBM((length * tiles, LANES), f32)],
        [
            message_scratch,
            scan_scratch,
            state_scratch,
            state_scratch,
            dma((HALVES,)),
            dma((COPIES,)),
        ],
        4 * work,
    )(segments, cuts, feats, grad_scan, *squares, table, gain_table, adjoint)

    def local(backward, cuts, *sources):
        return call(
            lambda *refs: local_kernel(backward, *refs),
            "local_backward" if backward else "local_forward",
            [smem, smem] + ([hbm, hbm, hbm, vmem] if backward else [vmem, hbm, vmem]),
            [hbm, vmem, vmem] if backward else [vmem, hbm],
            [pltpu.HBM(wide, f32), here((1, length), f32), here(wide, jnp.bfloat16)]
            if backward
            else [here(wide, f32), pltpu.HBM(table.shape, f32)],
            [scan_scratch, dma((COPIES,))]
            + (
                [
                    pltpu.VMEM(wide, f32),
                    dma((HALVES,)),
                    pltpu.VMEM((length, LANES), f32),
                    pltpu.VMEM((length * tiles, LANES), f32),
                    dma((COPIES,)),
                    pltpu.VMEM(table.shape, f32),
                    dma((1,)),
                ]
                if backward
                else [scan_scratch, pltpu.VMEM(wide, jnp.bfloat16), dma((1,))]
            ),
            4 * work,
        )(segments, cuts, *sources)

    conv_local, late_table = local(False, cuts, table, raw[0], inverse)
    msg = exchange(msg)
    late_cuts, msg, conv_local = lax.optimization_barrier((cuts, msg, conv_local))

    own = lax.axis_index("ctx").astype(jnp.int32).reshape(1)
    back = call(
        lambda *refs: carry_kernel(length, norm_factor, *refs),
        "carries",
        [smem] + [vmem] * 4,
        hbm,
        message,
        [message_scratch, pltpu.VMEM((count, MODES, LANES), f32), dma((COPIES,))],
        32 * count * MODES * LANES,
    )(own, msg, rates.T, residue.T, gain_row)

    grad_local, inner_local, feats = local(
        True, late_cuts, *in_hbm(late_table, late_grad), raw[0], gain_row
    )
    back = exchange(back)

    matmuls = 3 * 2 * length * width * WIDE
    carried, inner, totals, gate, grad = call(
        backward_kernel,
        "backward",
        [smem] + [vmem] * 4 + [hbm] * 2,
        [vmem] * 5,
        [
            here(wide, f32),
            here((1, length), f32),
            here((count, LANES), f32),
            here(wide, jnp.bfloat16),
            here(wide, jnp.bfloat16),
        ],
        [pltpu.VMEM((length, LANES), f32), dma((2, COPIES))],
        matmuls,
    )(cuts, back, inner_local, feats, gain_row, raw[1], raw[2])
    inner = all_parts(inner)
    other = lax.ppermute(totals, "dp", [(i, (i + 1) % size) for i in range(size)])

    mixed, grad_gate = call(
        forward_kernel,
        "forward",
        [smem] + [vmem] * 5,
        [vmem] * 2,
        [here(wide, jnp.bfloat16)] * 2,
        [pltpu.VMEM(wide, f32)],
        matmuls,
    )(cuts, back, conv_local, gate, grad, gain_row)

    grad_features, grad_residue, grad_gain, mixed, grad_gate = call(
        lambda *refs: feature_kernel(full_width, *refs),
        "features",
        [vmem] * 13,
        [hbm, vmem, vmem, hbm, hbm],
        [
            jax.ShapeDtypeStruct(wide, jnp.bfloat16),
            jax.ShapeDtypeStruct((mode_count, group_count), f32),
            jax.ShapeDtypeStruct((tiles, LANES), f32),
            jax.ShapeDtypeStruct(wide, jnp.bfloat16),
            jax.ShapeDtypeStruct(wide, jnp.bfloat16),
        ],
        [pltpu.VMEM(wide, jnp.bfloat16), dma((COPIES,)), dma((2, COPIES))],
        4 * length * width,
    )(grad_local, carried, feats, gain_row, inverse, *inner, totals, other, mixed, grad_gate)
    return (
        mixed[None],
        grad_features[None],
        grad_gate[None],
        grad_residue.T,
        grad_gain.reshape(width),
    )


def solution(mesh):
    placed = (
        P("dp", "ctx", "tensor"),
        P("dp", "ctx", "tensor"),
        P("dp", "ctx"),
        P("tensor"),
        P("tensor", None),
        P("tensor", None),
        P("dp", "ctx", "tensor"),
    )
    return jax.shard_map(
        shards,
        mesh=mesh,
        in_specs=placed,
        out_specs=(
            P("dp", "ctx", "tensor"),
            P("dp", "ctx", "tensor"),
            P("dp", "ctx", "tensor"),
            P("tensor", None),
            P("tensor"),
        ),
        check_vma=False,
    )
```

```python
import math

import jax
import jax.numpy as jnp
from jax import lax
from jax.experimental import pallas as pl
from jax.experimental.pallas import tpu as pltpu
from jax.sharding import PartitionSpec as P

epsilon = 1e-06
LANES = 128
TILES = 8
HALVES = 2
MODES = 16
GROUP = 16
UNROLL = 16
COUNT = 4
COPIES = 2
BLOCKS = 8
WIDE = 2 * LANES
ROWS = MODES + 2
HIGHEST = lax.Precision.HIGHEST
f32 = jnp.float32


def lane_iota(rows):
    return lax.broadcasted_iota(jnp.int32, (rows, LANES), 1)


def swap(value):
    return pltpu.roll(value, LANES // 2, axis=1)


def join(low, high):
    return jnp.where(lane_iota(low.shape[0]) < LANES // 2, low, high)


def total_row(parts):
    return tree([part[...] for part in parts])


def inverse_of(parts, full_width):
    return lax.rsqrt(total_row(parts) / full_width + epsilon)


def column(row):
    length = row.shape[1]
    row = jnp.broadcast_to(row, (8, length))
    return jnp.broadcast_to(jnp.transpose(row)[:, 0:1], (length, LANES))


def block_ones():
    left = lax.broadcasted_iota(jnp.int32, (LANES, LANES), 0) // GROUP
    right = lax.broadcasted_iota(jnp.int32, (LANES, LANES), 1) // GROUP
    return jnp.where(left == right, 1.0, 0.0).astype(jnp.bfloat16)


def exact_dot(value, ones):
    high = value.astype(jnp.bfloat16).astype(f32)
    middle = (value - high).astype(jnp.bfloat16).astype(f32)
    parts = jnp.concatenate([high, middle, value - high - middle], axis=0)
    full = jnp.dot(parts.astype(jnp.bfloat16), ones, preferred_element_type=f32)
    rows = value.shape[0]
    return full[0:rows] + (full[rows : 2 * rows] + full[2 * rows :])


def lanes_of(half, tile):
    return pl.ds(pl.multiple_of((half * TILES + tile) * LANES, LANES), LANES)


def tile_of(ref, half, tile):
    return ref[:, lanes_of(half, tile)].astype(f32)


def scan_rows(half, tile, length):
    return pl.ds(half * length * TILES + tile, length, stride=TILES)


def table_of(table, half, first):
    at = pl.ds(pl.multiple_of(half * TILES, TILES), TILES)
    return [table[first + r, at, :] for r in range(MODES)]


def decay_of(table, half):
    return [jnp.exp(-rate) for rate in table_of(table, half, 0)]


def weight_of(table, half):
    return table_of(table, half, MODES)


def state_rows(half, r):
    return pl.ds(half * TILES * MODES + r, TILES, stride=MODES)


def tree(values):
    values = list(values)
    while len(values) > 1:
        values = [a + b for a, b in zip(values[::2], values[1::2])]
    return values[0]


def scan(length, seg, cuts, step, carry, backward):
    groups = length // UNROLL

    def run(group, carry, masked):
        base = group * UNROLL
        for u in range(UNROLL):
            t = base + (UNROLL - 1 - u if backward else u)
            keep = None
            if masked:
                near = jnp.minimum(t + 1, length - 1) if backward else jnp.maximum(t - 1, 0)
                keep = seg[0, t] == seg[0, near]
            carry = step(t, carry, keep)
        return carry

    def stretch(p, carry):
        now, states = carry
        if backward:
            cut = jnp.where(p < COUNT - 1, cuts[jnp.maximum(COUNT - 2 - p, 0)], 0)
            group = (cut - 1) // UNROLL
            stop = jnp.where(
                cut >= length, now, jnp.where(cut <= 0, 0, jnp.minimum(now, group + 1))
            )
            states = lax.fori_loop(
                0, now - stop, lambda i, value: run(now - 1 - i, value, False), states
            )
            broken = (cut > 0) & (cut < length) & (group < now)
            after = group
        else:
            cut = jnp.where(p < COUNT - 1, cuts[jnp.minimum(p, COUNT - 2)], length)
            group = cut // UNROLL
            stop = jnp.where(
                cut <= 0, now, jnp.where(cut >= length, groups, jnp.maximum(now, group))
            )
            states = lax.fori_loop(now, stop, lambda i, value: run(i, value, False), states)
            broken = (cut > 0) & (cut < length) & (group >= now)
            after = group + 1
        states = lax.cond(
            broken, lambda value: run(group, value, True), lambda value: value, states
        )
        return jnp.where(broken, after, stop), states

    def general(carry):
        start = jnp.int32(groups if backward else 0)
        return lax.fori_loop(0, COUNT, stretch, (start, carry))[1]

    def unbroken(carry):
        def body(i, carry):
            return run(groups - 1 - i if backward else i, carry, False)

        return lax.fori_loop(0, groups, body, carry)

    broken = cuts[0] < 0
    for p in range(COUNT - 1):
        broken = broken | ((cuts[p] > 0) & (cuts[p] < length))
    return lax.cond(broken, general, unbroken, carry)


def decayed(decay, state, keep):
    state = decay * state
    return state if keep is None else jnp.where(keep, state, 0.0)


def row_at(ref, half, length, t):
    return ref[pl.ds(pl.multiple_of((half * length + t) * TILES, TILES), TILES), :]


def lane_sums(value):
    high = value.astype(jnp.bfloat16)
    rest = value - high.astype(f32)
    middle = rest.astype(jnp.bfloat16)
    low = (rest - middle.astype(f32)).astype(jnp.bfloat16)
    ones = jnp.ones((16, LANES), jnp.bfloat16)
    sums = [
        lax.dot_general(ones, part, (((1,), (1,)), ((), ())), preferred_element_type=f32)
        for part in (high, middle, low)
    ]
    return (sums[0] + (sums[1] + sums[2]))[0:1]


def load_kernel(
    feats_in, gate_in, grad_in, rates_in, residue_in, seg_in,
    feats, grad_scan, squares, table, rates_out, cuts,
    gate, grad, rates, residue, seg, sems, small_sems,
):
    length, width = feats.shape
    small = [
        pltpu.make_async_copy(src, dst, small_sems.at[n])
        for n, (src, dst) in enumerate(((rates_in, rates), (residue_in, residue), (seg_in, seg)))
    ]
    for copy in small:
        copy.start()
    feat_copies = row_copies(feats_in, feats, sems.at[0])
    copies = row_copies(gate_in, gate, sems.at[1]) + row_copies(grad_in, grad, sems.at[2])
    for copy in small:
        copy.wait()
    expand(rates, residue, seg, table, cuts)
    rates_out[...] = rates[...]
    wait_all(feat_copies)
    partial = jnp.zeros((length, LANES), f32)
    for tile in range(width // LANES):
        value = tile_of(feats, 0, tile)
        partial = partial + value * value
    squares[...] = lane_sums(partial)
    wait_all(copies)
    for half in range(HALVES):
        for tile in range(TILES):
            value = tile_of(gate, half, tile) * tile_of(grad, half, tile)
            grad_scan[scan_rows(half, tile, length), :] = value


def mode_params(rates, residue):
    rate = rates[...]
    twice = 2.0 * rate
    series = 1.0 - twice / 6.0
    for n in (5, 4, 3, 2):
        series = 1.0 - twice / n * series
    root = jnp.sqrt(jnp.where(twice < 0.25, twice * series, 1.0 - jnp.exp(-twice)))
    return jnp.concatenate([rate, residue[...] * root, root], axis=0)


def spread_groups(packed, width, first):
    group_count = packed.shape[1]
    group = lax.broadcasted_iota(jnp.int32, (group_count, width), 0)
    lane = lax.broadcasted_iota(jnp.int32, (group_count, width), 1)
    spread = jnp.where(first(lane) == group, 1.0, 0.0).astype(jnp.bfloat16)
    return exact_dot(packed, spread)


def own_mode(value):
    row = lax.broadcasted_iota(jnp.int32, value.shape, 0)
    lane = lax.broadcasted_iota(jnp.int32, value.shape, 1)
    return jnp.sum(jnp.where(row == lane % GROUP, value, 0.0), axis=0, keepdims=True)


def expand(rates, residue, seg, table, cuts):
    width = table.shape[1] * LANES
    full = spread_groups(mode_params(rates, residue), width, lambda lane: lane // GROUP)
    for tile in range(width // LANES):
        at = slice(tile * LANES, (tile + 1) * LANES)
        table[:, tile, :] = full[0 : 2 * MODES, at]
    for p in range(COUNT - 1):
        cuts[p] = jnp.sum(jnp.where(seg[...] <= p, 1, 0))
    cuts[COUNT - 1] = seg.shape[1]


def adjoint_kernel(cuts, grad_scan, rates, adj):
    length = grad_scan.shape[0] // (HALVES * TILES)
    edge = jnp.int32(length)
    for p in range(COUNT - 1):
        edge = jnp.minimum(edge, jnp.where(cuts[p] > 0, cuts[p], length))
    first = lax.broadcasted_iota(jnp.int32, (length, LANES), 0) < edge
    lag = lax.broadcasted_iota(jnp.int32, (MODES, LANES), 1).astype(f32)
    rate = rates[...]
    further = jnp.exp(-float(LANES) * rate)
    share = LANES // GROUP
    row = lax.broadcasted_iota(jnp.int32, (LANES, LANES), 0) // MODES
    own = row == lax.broadcasted_iota(jnp.int32, (LANES, LANES), 1) // GROUP
    dot = lambda x, y: jnp.dot(x, y, preferred_element_type=f32)
    for tile in range(HALVES * TILES):
        value = grad_scan[scan_rows(tile // TILES, tile % TILES, length), :]
        high, low = split(jnp.where(first, value, 0.0))
        blocks = []
        for group in range(tile * share, (tile + 1) * share):
            parts = [jnp.exp(-lag * rate[:, group : group + 1])]
            for _ in range(length // LANES - 1):
                parts.append(parts[-1] * further[:, group : group + 1])
            blocks.append(jnp.concatenate(parts, axis=1))
        near, far = split(jnp.concatenate(blocks, axis=0))
        full = dot(near, high) + (dot(far, high) + dot(near, low))
        full = jnp.where(own, full, 0.0)
        adj[tile * MODES : (tile + 1) * MODES, :] = tree(
            [full[n * MODES : (n + 1) * MODES, :] for n in range(share)]
        )


def state_kernel(
    full_width, seg, cuts, feats, grad_scan, part0, part1, part2, part3, table, gain, adj,
    msg_out, inverse, grad_out, msg, feat_scan, ends, sums, sems, grad_sems,
):
    length = feats.shape[0]
    grad_copies = row_copies(grad_scan, grad_out, grad_sems)
    inverse[...] = inverse_of((part0, part1, part2, part3), full_width)
    scale = column(inverse[...])
    share = msg.shape[0] // HALVES

    def send(half):
        at = pl.ds(half * share, share)
        return pltpu.make_async_copy(msg.at[at, :], msg_out.at[at, :], sems.at[half])

    for half in range(HALVES):
        state_half(
            length, half, scale, seg, cuts, feats, grad_scan, table, gain, adj,
            msg, feat_scan, ends, sums,
        )
        send(half).start()
    for half in range(HALVES):
        send(half).wait()
    wait_all(grad_copies)


def state_half(
    length, half, scale, seg, cuts, feats, grad_scan, table, gain, adj,
    msg, feat_scan, ends, sums,
):
    for tile in range(TILES):
        feat_scan[scan_rows(0, tile, length), :] = tile_of(feats, half, tile) * scale
    decay = decay_of(table, half)

    def step(t, carry, keep):
        value = row_at(feat_scan, 0, length, t)
        grads = row_at(grad_scan, half, length, t)
        states = [decayed(decay[r], carry[r], keep) + value for r in range(MODES)]
        totals = [carry[MODES + r] + grads * states[r] for r in range(MODES)]
        return tuple(states) + tuple(totals)

    zero = jnp.zeros((TILES, LANES), f32)
    carry = scan(length, seg, cuts, step, (zero,) * (2 * MODES), False)
    gains = gain[pl.ds(pl.multiple_of(half * TILES, TILES), TILES), :]
    weights = weight_of(table, half)
    for r in range(MODES):
        ends[pl.ds(r, TILES, stride=MODES), :] = carry[r]
        sums[r * TILES : (r + 1) * TILES, :] = carry[MODES + r] * gains
    gain_row = tree([weights[r] * carry[MODES + r] for r in range(MODES)])
    spread = exact_dot(sums[...], block_ones())
    lane_mode = lane_iota(TILES) % GROUP
    mode_row = tree(
        [
            jnp.where(lane_mode == r, spread[r * TILES : (r + 1) * TILES, :], 0.0)
            for r in range(MODES)
        ]
    )
    even = join(gain_row, swap(mode_row))
    odd = join(swap(gain_row), mode_row)
    first = jnp.full((1, LANES), seg[0, 0], jnp.int32).astype(f32)
    last = jnp.full((1, LANES), seg[0, length - 1], jnp.int32).astype(f32)
    near = join(first, last)

    for tile in range(TILES):
        state = ends[tile * MODES : (tile + 1) * MODES, :]
        own = (half * TILES + tile) * MODES
        adjoint = adj[pl.ds(pl.multiple_of(own, MODES), MODES), :]
        at = 2 * (half * TILES + tile) * ROWS
        msg[at : at + MODES, :] = join(state, swap(adjoint))
        msg[at + MODES : at + MODES + 1, :] = even[tile : tile + 1, :]
        msg[at + MODES + 1 : at + ROWS, :] = near
        at += ROWS
        msg[at : at + MODES, :] = join(swap(state), adjoint)
        msg[at + MODES : at + MODES + 1, :] = odd[tile : tile + 1, :]
        msg[at + MODES + 1 : at + ROWS, :] = near


def carry_kernel(
    span, norm_factor, own, msg, rates, residue, gain, out_hbm, out, carries, sems
):
    count = msg.shape[0] // ROWS
    share = rates.shape[1] // count
    first = own[0] * share
    full = spread_groups(
        mode_params(rates, residue), LANES, lambda lane: first + lane % (LANES // 2) // GROUP
    )
    rate, weight = full[0:MODES], full[MODES : 2 * MODES]
    root = own_mode(full[2 * MODES :])
    at = pl.ds(pl.multiple_of(own[0] // 2 * LANES, LANES), LANES)
    gains = gain[:, at]
    odd = own[0] % 2 == 1
    gains = jnp.where(odd, join(swap(gains), gains), join(gains, swap(gains)))
    single = jnp.exp(-rate)
    whole = jnp.exp(-rate * float(span))
    state = jnp.zeros((MODES, LANES), f32)
    before = None
    ends = [msg[i * ROWS : i * ROWS + MODES, :] for i in range(count)]
    ids = [msg[i * ROWS + MODES + 1 : (i + 1) * ROWS, :] for i in range(count)]
    for m in range(count):
        other = count - 1 - m
        fresh = join(ends[m], ends[other])
        near = join(ids[m], ids[other])
        far = join(swap(ids[m]), swap(ids[other]))
        if before is None:
            carries[m] = state
            state = fresh
        else:
            carries[m] = jnp.where(near == before, state, 0.0)
            state = fresh + jnp.where(far == before, whole * state, 0.0)
        before = far
    total = jnp.zeros((MODES, LANES), f32)
    row = jnp.zeros((1, LANES), f32)
    for i in range(count):
        carried = join(carries[i], carries[count - 1 - i])
        out[i * ROWS : i * ROWS + MODES, :] = carried
        total = total + carried * swap(ends[i])
        row = row + msg[i * ROWS + MODES : i * ROWS + MODES + 1, :]
    total = total * single
    gain_row = jnp.sum(weight * total, axis=0, keepdims=True)
    spread = exact_dot(total * gains, block_ones())
    pick = lane_iota(MODES) % GROUP == lax.broadcasted_iota(jnp.int32, (MODES, LANES), 0)
    mode_row = jnp.sum(jnp.where(pick, spread, 0.0), axis=0, keepdims=True)
    row = (row + join(gain_row, swap(mode_row))) * join(jnp.ones((1, LANES), f32), root)
    row = row * norm_factor
    modes = join(own_mode(rate), own_mode(weight))
    for i in range(count):
        out[i * ROWS + MODES : i * ROWS + MODES + 1, :] = row
        out[i * ROWS + MODES + 1 : (i + 1) * ROWS, :] = modes
    copies = []
    part = out.shape[0] // COPIES
    for i in range(COPIES):
        at = pl.ds(i * part, part)
        copies.append(pltpu.make_async_copy(out.at[at, :], out_hbm.at[at, :], sems.at[i]))
        copies[-1].start()
    for copy in copies:
        copy.wait()


def local_kernel(backward, seg, cuts, table_in, *refs):
    if backward:
        grad_in, feats_in, gain, out, inner, feats, result, feat_sems, *rest = refs
        value_out, sems, partial, grad_scan, grad_sems, table, table_sem = rest
        table_copy = pltpu.make_async_copy(table_in, table, table_sem.at[0])
        table_copy.start()
        grad_copies = row_copies(grad_in, grad_scan, grad_sems)
    else:
        feats_in, inverse, value_out, table_out, result, feat_sems, scan_in, feats, table_sem = refs
        table = table_in
        table_copy = pltpu.make_async_copy(table, table_out, table_sem.at[0])
        table_copy.start()
    length = seg.shape[1]
    feat_copies = row_copies(feats_in, feats, feat_sems)
    if not backward:
        scale = column(inverse[...])
        wait_all(feat_copies)
    copies = []
    for half in range(HALVES):
        if backward:
            values, at_half = grad_scan, half
            part = COPIES // HALVES
            wait_all(grad_copies[half * part : (half + 1) * part])
            if half == 0:
                table_copy.wait()
        else:
            values, at_half = scan_in, 0
            for tile in range(TILES):
                values[scan_rows(0, tile, length), :] = tile_of(feats, half, tile) * scale
        decay = decay_of(table, half)
        weight = weight_of(table, half)

        def step(t, states, keep):
            value = row_at(values, at_half, length, t)
            states = tuple(decayed(decay[r], states[r], keep) + value for r in range(MODES))
            result[pl.ds(pl.multiple_of(t * TILES, TILES), TILES), :] = tree(
                [weight[r] * states[r] for r in range(MODES)]
            )
            return states

        zero = jnp.zeros((TILES, LANES), f32)
        scan(length, seg, cuts, step, (zero,) * MODES, backward)
        for tile in range(TILES):
            value_out[:, lanes_of(half, tile)] = result[pl.ds(tile, length, stride=TILES), :]
        if backward:
            at = pl.ds(half * TILES * LANES, TILES * LANES)
            copies.append(pltpu.make_async_copy(value_out.at[:, at], out.at[:, at], sems.at[half]))
            copies[-1].start()
    if backward:
        wait_all(feat_copies)
        inner[...] = inner_sums(value_out, feats, gain, partial)
    else:
        table_copy.wait()
    wait_all(copies)


def inner_sums(value, feats, gain, partial):
    length, width = feats.shape
    step = length // BLOCKS
    for i in range(BLOCKS):
        here = slice(i * step, (i + 1) * step)
        partial[here, :] = tree(
            [
                value[here, at] * gain[:, at] * feats[here, at].astype(f32)
                for at in tiles_at(width)
            ]
        )
    return lane_sums(partial[...])


def from_owners(back, pair, rows, upper):
    parts = []
    for n in range(2):
        first = (4 * pair + 2 * n) * ROWS
        low = back[first + rows.start : first + rows.stop, :]
        high = back[first + ROWS + rows.start : first + ROWS + rows.stop, :]
        parts.append(join(swap(low), high) if upper else join(low, swap(high)))
    return jnp.concatenate(parts, axis=1)


def powers(cuts, back, pair, length, ahead):
    t = lax.broadcasted_iota(jnp.int32, (length, WIDE), 0)
    modes = slice(MODES + 1, MODES + 2)
    rate = from_owners(back, pair, modes, False)
    weight = from_owners(back, pair, modes, True)
    sub = lax.broadcasted_iota(jnp.int32, (8, WIDE), 0).astype(f32)
    further = jnp.exp(-8.0 * rate)
    if ahead:
        edge = jnp.int32(0)
        for p in range(COUNT - 1):
            edge = jnp.maximum(edge, jnp.where(cuts[p] < length, cuts[p], 0))
        linked = t >= edge
        lag = 8.0 - sub
    else:
        edge = jnp.int32(length)
        for p in range(COUNT - 1):
            edge = jnp.minimum(edge, jnp.where(cuts[p] > 0, cuts[p], length))
        linked = t < edge
        lag = sub + 1.0
    blocks = [jnp.exp(-lag * rate) * weight]
    for _ in range(length // 8 - 1):
        blocks.append(blocks[-1] * further)
    power = jnp.concatenate(blocks[::-1] if ahead else blocks, axis=0)
    return split(jnp.where(linked, power, 0.0))


def split(value):
    high = value.astype(jnp.bfloat16)
    return high, (value - high.astype(f32)).astype(jnp.bfloat16)


def from_carry(cuts, back, pair, length, ahead):
    carry = from_owners(back, pair, slice(0, MODES), ahead)
    own = lax.broadcasted_iota(jnp.int32, (WIDE, WIDE), 0) // MODES == (
        lax.broadcasted_iota(jnp.int32, (WIDE, WIDE), 1) // GROUP
    )

    def spread(value):
        value = jnp.concatenate([value.astype(f32)] * (WIDE // MODES), axis=0)
        return jnp.where(own, value, 0.0).astype(jnp.bfloat16)

    high, low = (spread(value) for value in split(carry))
    near, far = powers(cuts, back, pair, length, ahead)
    dot = lambda x, y: jnp.dot(x, y, preferred_element_type=f32)
    return dot(near, high) + (dot(far, high) + dot(near, low))


def row_copy(src, dst, sems, part, parts=COPIES):
    step = dst.shape[0] // parts
    at = pl.ds(part * step, step)
    return pltpu.make_async_copy(src.at[at, :], dst.at[at, :], sems.at[part])


def row_copies(src, dst, sems, parts=COPIES):
    copies = [row_copy(src, dst, sems, part, parts) for part in range(parts)]
    for copy in copies:
        copy.start()
    return copies


def wait_all(copies):
    for copy in copies:
        copy.wait()


def tiles_at(width):
    return [slice(tile * LANES, (tile + 1) * LANES) for tile in range(width // LANES)]


def backward_kernel(
    cuts, back, inner_local, feats, gain, gate_in, grad_in,
    carried, inner, totals, gate, grad, partial, sems,
):
    length, width = feats.shape
    copies = []
    for n, (src, dst) in enumerate(((gate_in, gate), (grad_in, grad))):
        copies += row_copies(src, dst, sems.at[n], 1)
    for n in range(totals.shape[0]):
        totals[n : n + 1, :] = back[n * ROWS + MODES : n * ROWS + MODES + 1, :]
    for pair in range(width // WIDE):
        at = slice(pair * WIDE, (pair + 1) * WIDE)
        carried[:, at] = from_carry(cuts, back, pair, length, True)
    inner[...] = inner_local[...] + inner_sums(carried, feats, gain, partial)
    wait_all(copies)


def forward_kernel(
    cuts, back, local, gate, grad, gain, mixed, grad_gate, carried
):
    length, width = gate.shape
    for pair in range(width // WIDE):
        at = slice(pair * WIDE, (pair + 1) * WIDE)
        carried[:, at] = from_carry(cuts, back, pair, length, False)
    step = length // BLOCKS
    for i in range(BLOCKS):
        here = slice(i * step, (i + 1) * step)
        for at in tiles_at(width):
            conv = (local[here, at] + carried[here, at]) * gain[:, at]
            mixed[here, at] = (gate[here, at].astype(f32) * conv).astype(jnp.bfloat16)
            grad_gate[here, at] = (grad[here, at].astype(f32) * conv).astype(jnp.bfloat16)


def feature_kernel(
    full_width, local, carried, feats, gain, inverse, i0, i1, i2, i3, own, other, mixed_v, grad_gate_v,
    out, modes, gains, mixed, grad_gate, out_v, sems, gate_sems,
):
    length, width = feats.shape
    gate_copies = row_copies(mixed_v, mixed, gate_sems.at[0])
    gate_copies += row_copies(grad_gate_v, grad_gate, gate_sems.at[1])
    scale = column(inverse[...])
    factor = column(total_row((i0, i1, i2, i3))) * scale * scale / full_width
    copies = []
    step = length // BLOCKS
    for i in range(BLOCKS):
        here = slice(i * step, (i + 1) * step)
        for at in tiles_at(width):
            scaled = (local[here, at] + carried[here, at]) * gain[:, at]
            value = scale[here] * (scaled - feats[here, at].astype(f32) * factor[here])
            out_v[here, at] = value.astype(jnp.bfloat16)
        if (i + 1) % (BLOCKS // COPIES) == 0:
            copies.append(row_copy(out_v, out, sems, (i + 1) // (BLOCKS // COPIES) - 1))
            copies[-1].start()

    total = own[...] + other[...]
    count = total.shape[0]
    groups = modes.shape[1]
    share = groups // count
    slot = lax.broadcasted_iota(jnp.int32, (count, groups), 1) // share
    pick = jnp.where(slot == lax.broadcasted_iota(jnp.int32, (count, groups), 0), 1.0, 0.0)
    spread = lax.dot_general(
        total,
        pick.astype(f32),
        (((0,), (0,)), ((), ())),
        precision=HIGHEST,
        preferred_element_type=f32,
    )
    member = lax.broadcasted_iota(jnp.int32, (MODES, groups), 1) % share
    parts = [
        jnp.where(member == n, spread[LANES // 2 + n * MODES : LANES // 2 + (n + 1) * MODES], 0.0)
        for n in range(share)
    ]
    modes[...] = tree(parts)
    for n in range(count // 2):
        gains[n : n + 1, :] = join(total[2 * n : 2 * n + 1, :], swap(total[2 * n + 1 : 2 * n + 2, :]))
    wait_all(copies + gate_copies)


def all_parts(value):
    size = lax.axis_size("tensor")
    others = [
        lax.ppermute(value, "tensor", [(i, (i + d) % size) for i in range(size)])
        for d in range(1, size)
    ]
    return [value] + others


def shards(features, gate_in, segments, gain, residue, rates, grad_out):
    _, length, width = features.shape
    group_count, mode_count = rates.shape
    count = lax.axis_size("ctx")
    full_width = width * lax.axis_size("tensor")
    size = lax.axis_size("dp")
    norm_factor = 1.0 / math.sqrt(size * length * count)
    tiles = width // LANES
    gain_table = gain.reshape(tiles, LANES)
    gain_row = gain.reshape(1, width)

    smem = pl.BlockSpec(memory_space=pltpu.SMEM)
    vmem = pl.BlockSpec(memory_space=pltpu.VMEM)
    hbm = pl.BlockSpec(memory_space=pl.ANY)
    here = pltpu.VMEM
    work = length * width * MODES
    wide = (length, width)
    scan_shape = here((length * tiles, LANES), f32)
    message = pltpu.HBM((count * ROWS, LANES), f32)

    def exchange(value):
        value = value.reshape(count, 1, ROWS * LANES)
        return lax.all_to_all(value, "ctx", 0, 0, tiled=True).reshape(message.shape)

    state_scratch = pltpu.VMEM((TILES * MODES, LANES), f32)

    def call(kernel, name, in_specs, out_specs, out_shape, scratch, flops):
        return pl.pallas_call(
            kernel,
            in_specs=in_specs,
            out_specs=out_specs,
            out_shape=out_shape,
            scratch_shapes=scratch,
            compiler_params=pltpu.CompilerParams(vmem_limit_bytes=16 * 1024 * 1024),
            cost_estimate=pl.CostEstimate(
                flops=flops // 10**6, bytes_accessed=1, transcendentals=0
            ),
            name=name,
        )

    def in_hbm(*values):
        return [pltpu.with_memory_space_constraint(value, pltpu.HBM) for value in values]

    raw = in_hbm(features[0], gate_in[0], grad_out[0], rates.T, residue.T, segments)
    dma = pltpu.SemaphoreType.DMA
    feats, grad_scan, squares, table, rates_here, cuts = call(
        load_kernel,
        "load",
        [hbm] * 6,
        [vmem] * 5 + [smem],
        [
            here(wide, jnp.bfloat16),
            scan_shape,
            here((1, length), f32),
            here((2 * mode_count, tiles, LANES), f32),
            here((mode_count, group_count), f32),
            jax.ShapeDtypeStruct((COUNT,), jnp.int32),
        ],
        [
            pltpu.VMEM(wide, jnp.bfloat16),
            pltpu.VMEM(wide, jnp.bfloat16),
            pltpu.VMEM((mode_count, group_count), f32),
            pltpu.VMEM((mode_count, group_count), f32),
            pltpu.VMEM((1, length), jnp.int32),
            dma((3, COPIES)),
            dma((3,)),
        ],
        2 * length * width,
    )(*raw)
    squares = all_parts(squares)

    adjoint = call(
        adjoint_kernel,
        "adjoint",
        [smem] + [vmem] * 2,
        vmem,
        here((tiles * MODES, LANES), f32),
        [],
        2 * work,
    )(cuts, grad_scan, rates_here)

    scan_scratch = pltpu.VMEM((length * TILES, LANES), f32)
    message_scratch = pltpu.VMEM(message.shape, f32)
    msg, inverse, late_grad = call(
        lambda *refs: state_kernel(full_width, *refs),
        "states",
        [smem, smem] + [vmem] * 9,
        [hbm, vmem, hbm],
        [message, here((1, length), f32), pltpu.HBM((length * tiles, LANES), f32)],
        [
            message_scratch,
            scan_scratch,
            state_scratch,
            state_scratch,
            dma((HALVES,)),
            dma((COPIES,)),
        ],
        4 * work,
    )(segments, cuts, feats, grad_scan, *squares, table, gain_table, adjoint)

    def local(backward, cuts, *sources):
        return call(
            lambda *refs: local_kernel(backward, *refs),
            "local_backward" if backward else "local_forward",
            [smem, smem] + ([hbm, hbm, hbm, vmem] if backward else [vmem, hbm, vmem]),
            [hbm, vmem, vmem] if backward else [vmem, hbm],
            [pltpu.HBM(wide, f32), here((1, length), f32), here(wide, jnp.bfloat16)]
            if backward
            else [here(wide, f32), pltpu.HBM(table.shape, f32)],
            [scan_scratch, dma((COPIES,))]
            + (
                [
                    pltpu.VMEM(wide, f32),
                    dma((HALVES,)),
                    pltpu.VMEM((length, LANES), f32),
                    pltpu.VMEM((length * tiles, LANES), f32),
                    dma((COPIES,)),
                    pltpu.VMEM(table.shape, f32),
                    dma((1,)),
                ]
                if backward
                else [scan_scratch, pltpu.VMEM(wide, jnp.bfloat16), dma((1,))]
            ),
            4 * work,
        )(segments, cuts, *sources)

    conv_local, late_table = local(False, cuts, table, raw[0], inverse)
    msg = exchange(msg)
    late_cuts, msg, conv_local = lax.optimization_barrier((cuts, msg, conv_local))

    own = lax.axis_index("ctx").astype(jnp.int32).reshape(1)
    back = call(
        lambda *refs: carry_kernel(length, norm_factor, *refs),
        "carries",
        [smem] + [vmem] * 4,
        hbm,
        message,
        [message_scratch, pltpu.VMEM((count, MODES, LANES), f32), dma((COPIES,))],
        32 * count * MODES * LANES,
    )(own, msg, rates.T, residue.T, gain_row)

    grad_local, inner_local, feats = local(
        True, late_cuts, *in_hbm(late_table, late_grad), raw[0], gain_row
    )
    back = exchange(back)

    matmuls = 3 * 2 * length * width * WIDE
    carried, inner, totals, gate, grad = call(
        backward_kernel,
        "backward",
        [smem] + [vmem] * 4 + [hbm] * 2,
        [vmem] * 5,
        [
            here(wide, f32),
            here((1, length), f32),
            here((count, LANES), f32),
            here(wide, jnp.bfloat16),
            here(wide, jnp.bfloat16),
        ],
        [pltpu.VMEM((length, LANES), f32), dma((2, COPIES))],
        matmuls,
    )(cuts, back, inner_local, feats, gain_row, raw[1], raw[2])
    inner = all_parts(inner)
    other = lax.ppermute(totals, "dp", [(i, (i + 1) % size) for i in range(size)])

    mixed, grad_gate = call(
        forward_kernel,
        "forward",
        [smem] + [vmem] * 5,
        [vmem] * 2,
        [here(wide, jnp.bfloat16)] * 2,
        [pltpu.VMEM(wide, f32)],
        matmuls,
    )(cuts, back, conv_local, gate, grad, gain_row)

    grad_features, grad_residue, grad_gain, mixed, grad_gate = call(
        lambda *refs: feature_kernel(full_width, *refs),
        "features",
        [vmem] * 13,
        [hbm, vmem, vmem, hbm, hbm],
        [
            jax.ShapeDtypeStruct(wide, jnp.bfloat16),
            jax.ShapeDtypeStruct((mode_count, group_count), f32),
            jax.ShapeDtypeStruct((tiles, LANES), f32),
            jax.ShapeDtypeStruct(wide, jnp.bfloat16),
            jax.ShapeDtypeStruct(wide, jnp.bfloat16),
        ],
        [pltpu.VMEM(wide, jnp.bfloat16), dma((COPIES,)), dma((2, COPIES))],
        4 * length * width,
    )(grad_local, carried, feats, gain_row, inverse, *inner, totals, other, mixed, grad_gate)
    return (
        mixed[None],
        grad_features[None],
        grad_gate[None],
        grad_residue.T,
        grad_gain.reshape(width),
    )


def solution(mesh):
    placed = (
        P("dp", "ctx", "tensor"),
        P("dp", "ctx", "tensor"),
        P("dp", "ctx"),
        P("tensor"),
        P("tensor", None),
        P("tensor", None),
        P("dp", "ctx", "tensor"),
    )
    return jax.shard_map(
        shards,
        mesh=mesh,
        in_specs=placed,
        out_specs=(
            P("dp", "ctx", "tensor"),
            P("dp", "ctx", "tensor"),
            P("dp", "ctx", "tensor"),
            P("tensor", None),
            P("tensor"),
        ),
        check_vma=False,
    )
```
